512 devices in a mesh: acq: 16 (over y, core), az: 32 (over x, z).
Axes of the slice: x: 4, y: 8, z: 8, core: 2. Of those that a mesh axis runs over, the one named last changes fastest.
Arguments:
- complex_slabs: bfloat16 [96, 2, 320, 2560], P('acq', None, 'az'), may hold values from -1250 to 1250
- secondaries: int32 [96, 10], P('acq'), may hold values from 1 to 95, as said below
- pair_counts: int32 [96], P('acq'), may hold values from 0 to 10, as said below
- phase_screens: float32 [96, 64, 128], P(None, 'az'), may hold values from -3.140625 to 3.140625
Outputs:
- screen_gradient: float32 [96, 64, 128], P('acq', 'az')
- pair_misfit: float32 [96, 64, 128], P('acq', 'az')
The draws below stay inside these ranges and needn't reach their ends.
Inputs may be any that keep to these rules, and one draw needn't show every extreme that they name: `secondaries`: for every acquisition a, the first pair_counts[a] entries of row a are distinct acquisitions from a + 1 to a + 12; the remaining entries are ignored. pair_counts[a] <= min(10, 95 - a).
All inputs are finite; a program needn't handle non-finite values.
Results may differ from the reference program's by a relative error of at most 0.0003.
Values may be sent and summed in bfloat16 or wider, within the bound.
A program may use at most 128 MiB of HBM per device.

```python
import math
import jax
import jax.numpy as jnp
from jax import lax

ACQ = 96
KMAX = 10
LAG = 12
LOOK_R = 5
LOOK_C = 20
ML_COLS = 128
COLS = 2560
ML_ROWS = 64
NROWS = 320


def pair_table(key):
    keys = jax.random.split(key, 2)
    requested = jax.random.randint(keys[0], (ACQ,), 4, KMAX + 1)
    acq_positions = jnp.arange(ACQ, dtype=jnp.int32)
    available = jnp.minimum(LAG, ACQ - 1 - acq_positions)
    counted = jnp.minimum(requested, available).at[0].set(KMAX)
    offsets = jnp.arange(LAG, dtype=jnp.int32)
    scores = jax.random.randint(keys[1], (ACQ, LAG), 0, 65536) * LAG + offsets[None, :]
    scores = jnp.where(offsets[None, :] < available[:, None], scores, scores + 4194304)
    ranking = jnp.argsort(scores, axis=1)[:, :KMAX].astype(jnp.int32)
    partner_table = jnp.minimum(acq_positions[:, None] + 1 + ranking, ACQ - 1)
    return (partner_table.astype(jnp.int32), counted.astype(jnp.int32))


def draw_secondaries(key, part):
    partner_table, counted = pair_table(key)
    return partner_table


def draw_pair_counts(key, part):
    partner_table, counted = pair_table(key)
    return counted


def draw_complex_slabs(key, part):
    key = jax.random.fold_in(key, 11)
    keys = jax.random.split(key, 5)
    shape_all = (ACQ, 2, NROWS, COLS)
    scene_field = jnp.clip(jax.random.normal(keys[0], (1, 2, NROWS, COLS)), -5.0, 5.0)
    speckle = jnp.clip(jax.random.normal(keys[1], shape_all), -5.0, 5.0)
    top_scale = 10.0
    coherent = jax.random.uniform(keys[2], (ACQ, 1, 1, 1), minval=0.3, maxval=1.5)
    row_scales = jnp.exp(jax.random.uniform(keys[3], (1, 1, NROWS, 1), minval=0.0, maxval=math.log(top_scale)))
    column_scales = jnp.exp(jax.random.uniform(keys[4], (1, 1, 1, COLS), minval=0.0, maxval=math.log(top_scale)))
    return (row_scales * column_scales * (coherent * scene_field + speckle)).astype(jnp.bfloat16)


def setup_inputs(seed: int = 0) -> dict:
    key_list = jax.random.split(jax.random.key(seed), 5)
    complex_slabs = draw_complex_slabs(jax.random.fold_in(key_list[4], 71), 0)
    secondaries = draw_secondaries(jax.random.fold_in(key_list[4], 71), 0)
    pair_counts = draw_pair_counts(jax.random.fold_in(key_list[4], 71), 0)
    phase_screens = jnp.clip(jax.random.uniform(key_list[3], (ACQ, ML_ROWS, ML_COLS), jnp.float32, -3.140625, 3.140625), -3.140625, 3.140625)
    return {"complex_slabs": complex_slabs, "secondaries": secondaries, "pair_counts": pair_counts, "phase_screens": phase_screens}


EPSILON = 1e-06

def multilook(samples):
    shifted = jnp.concatenate([jnp.zeros_like(samples[..., :2, :]), samples[..., :-2, :]], axis=-2)
    leading = samples.shape[:-2]
    blocks = shifted.reshape(leading + (samples.shape[-2] // LOOK_R, LOOK_R, samples.shape[-1] // LOOK_C, LOOK_C))
    return lax.optimization_barrier(jnp.sum(blocks, axis=(-3, -1)))

def intensity_of(acq_slab):
    widened = acq_slab.astype(jnp.float32)
    return multilook(widened[0] * widened[0] + widened[1] * widened[1])

def reference(complex_slabs, secondaries, pair_counts, phase_screens):
    power = lax.map(intensity_of, complex_slabs)

    def per_reference(gradient, reference_index):
        own_slab = complex_slabs[reference_index].astype(jnp.float32)
        own_power = power[reference_index]
        own_screen = phase_screens[reference_index]
        own_grad = jnp.zeros((ML_ROWS, ML_COLS), jnp.float32)
        misfit = jnp.zeros((ML_ROWS, ML_COLS), jnp.float32)
        for partner_slot in range(KMAX):
            partner_index = secondaries[reference_index, partner_slot]
            partner_slab = complex_slabs[partner_index].astype(jnp.float32)
            cross_real = multilook(own_slab[0] * partner_slab[0] + own_slab[1] * partner_slab[1])
            cross_imag = multilook(own_slab[1] * partner_slab[0] - own_slab[0] * partner_slab[1])
            normalizer = lax.rsqrt(own_power * power[partner_index] + EPSILON)
            screen_diff = own_screen - phase_screens[partner_index]
            cosine = jnp.cos(screen_diff)
            sine_part = jnp.sin(screen_diff)
            residual_real = normalizer * (cross_real * cosine + cross_imag * sine_part)
            residual_imag = normalizer * (cross_imag * cosine - cross_real * sine_part)
            active = (partner_slot < pair_counts[reference_index]).astype(jnp.float32)
            own_grad = own_grad - active * residual_imag
            misfit = misfit + active * (1.0 - residual_real)
            gradient = gradient.at[partner_index].add(active * residual_imag)
        gradient = gradient.at[reference_index].add(own_grad)
        return (gradient, misfit)
    start = jnp.zeros((ACQ, ML_ROWS, ML_COLS), jnp.float32)
    gradient, misfit = lax.scan(per_reference, start, jnp.arange(ACQ, dtype=jnp.int32))
    return (gradient, misfit)
```

```python
import functools

import jax
import jax.numpy as jnp
from jax import lax
from jax.experimental import pallas as pl
from jax.experimental.pallas import tpu as pltpu
from jax.sharding import PartitionSpec as P

EPSILON = 1e-6
MESH = pl.DeviceIdType.MESH
F32, BF16, I32 = jnp.float32, jnp.bfloat16, jnp.int32

ACQ = 6
OWN = 12
QUARTERS = 4
TILES = 5
GROUP = 2 * QUARTERS * ACQ
HALF = QUARTERS * ACQ
TOP, MID, RIM = 3 * GROUP, 5 * GROUP, 2 * GROUP


def slot_of(a):
    return a // ACQ * 8 + a % ACQ


def iota(shape, dim):
    return lax.broadcasted_iota(I32, shape, dim)


def kernel(
    chips, slabs,
    x_hbm, sec_ref, cnt_ref, screens_hbm,
    grad_ref, misfit_ref,
    xbuf, screens, perm, send, own, oth, ownf, masked, push, raw, red, comb, cross1, cross2,
    mytab, owntab, othtab, mypow, othpow, phi, trig, sums, msg_own, msg_oth, fin_own, fin_oth,
    load_sem, send_sem, recv_sem, small_send, small_recv,
):
    me = lax.axis_index("acq")
    az = lax.axis_index("az")
    y, core = me // 2, me % 2
    up = lax.rem(y + 1, chips)
    down = lax.rem(y + chips - 1, chips)
    az_next = lax.rem(az + 1, slabs)
    az_prev = lax.rem(az + slabs - 1, slabs)
    side = jnp.where(core == 0, up, down)
    back = jnp.where(core == 0, down, up)

    load_x = pltpu.make_async_copy(x_hbm, xbuf, load_sem.at[0])
    load_x.start()
    load_own = pltpu.make_async_copy(screens_hbm.at[pl.ds(OWN * y, OWN)], screens.at[0], load_sem.at[1])
    load_own.start()
    load_oth = pltpu.make_async_copy(screens_hbm.at[pl.ds(OWN * side, OWN)], screens.at[1], load_sem.at[2])
    load_oth.start()

    barrier = pltpu.get_barrier_semaphore()

    def greet(a, z):
        pl.semaphore_signal(barrier, inc=1, device_id=(a, z), device_id_type=MESH)

    greet(2 * y + 1 - core, az)
    for c in range(2):
        greet(2 * up + c, az)
        greet(2 * down + c, az)

    @pl.when(core == 0)
    def _():
        for c in range(2):
            greet(2 * y + c, az_prev)
            greet(2 * up + c, az_prev)

    row = iota((10 * GROUP, 128), 0)
    r = (row * 1366) >> 16
    rest = row - r * GROUP
    sixth = (rest * 10923) >> 16
    acq = rest - sixth * ACQ
    comp = sixth >> 2
    target = (sixth & 3) * (2 * ACQ * 16) + (acq * 2 + comp) * 16 + r
    lane = iota((10 * GROUP, 128), 1)
    for j in range(QUARTERS * 2 * ACQ * 16 // 128):
        perm[:, 128 * j : 128 * (j + 1)] = jnp.where(target == lane + 128 * j, 1.0, 0.0).astype(BF16)

    mytab[...] = jnp.full((8, 128), -1, I32)
    mytab[0:ACQ, 0:10] = sec_ref[...]
    slots = jnp.zeros((8, 128), I32)
    for i in range(ACQ):
        slots = jnp.where(iota((8, 128), 0) == i, cnt_ref[i], slots)
    mytab[...] = jnp.where(iota((8, 128), 1) < slots, mytab[...], -1)
    owntab[core] = mytab[...]

    pl.semaphore_wait(barrier, 7)

    def small(k, src, dst, a):
        return pltpu.make_async_remote_copy(
            src_ref=src, dst_ref=dst, send_sem=small_send.at[k], recv_sem=small_recv.at[k],
            device_id=(a, az), device_id_type=MESH,
        )

    def remote(t, k, first, rows, buffer, start, a, z, kind):
        return pltpu.make_async_remote_copy(
            src_ref=send.at[t, pl.ds(first, rows)],
            dst_ref=buffer.at[core, t, pl.ds(start, rows)],
            send_sem=send_sem.at[t, k],
            recv_sem=recv_sem.at[t, core, kind],
            device_id=(a, z), device_id_type=MESH,
        )

    def wide_copies(t):
        return (
            remote(t, 0, 0, TOP, oth, RIM, 2 * down, az, 0),
            remote(t, 1, TOP, MID, oth, 0, 2 * up + 1, az, 1),
            remote(t, 2, TOP + MID, RIM, oth, 0, 2 * down, az_next, 2),
            remote(t, 3, TOP + MID, RIM, own, 0, 2 * y, az_next, 3),
        )

    def chip_copy0(t):
        return remote(t, 4, TOP, MID, own, 0, 2 * y + 1, az, 4)

    def chip_copy1(t):
        return remote(t, 4, 0, TOP, own, RIM, 2 * y, az, 4)

    def arrived(t, block, kind, buffer, start, rows):
        pltpu.make_async_remote_copy(
            src_ref=send.at[t, pl.ds(0, rows)],
            dst_ref=buffer.at[block, t, pl.ds(start, rows)],
            send_sem=send_sem.at[t, 0],
            recv_sem=recv_sem.at[t, block, kind],
            device_id=(me, az), device_id_type=MESH,
        ).wait_recv()

    load_x.wait()

    tab_chip = small(0, mytab, owntab.at[core], 2 * y + 1 - core)
    tab_chip.start()

    def tab_up():
        return pltpu.make_async_remote_copy(
            src_ref=mytab, dst_ref=othtab.at[core], send_sem=small_send.at[1], recv_sem=small_recv.at[1 + core],
            device_id=(2 * up + 1, az), device_id_type=MESH,
        )

    tab_up().start()

    def repack(t, carry):
        parts = []
        for q in range(QUARTERS):
            lanes = pl.ds(pl.multiple_of(640 * q + 128 * t, 128), 128)
            for ac in range(2 * ACQ):
                parts.append(jnp.concatenate([xbuf[ac, :, lanes].astype(F32), jnp.zeros((6, 128), F32)], axis=0))
        stacked = jnp.concatenate(parts, axis=0).astype(BF16)
        send[t] = jnp.dot(perm[...], stacked, preferred_element_type=F32).astype(BF16)
        for copy in wide_copies(t):
            copy.start()

        @pl.when(core == 0)
        def _():
            chip_copy0(t).start()
            own[0, t, RIM:, :] = send[t, 0:TOP, :]

        @pl.when(core == 1)
        def _():
            chip_copy1(t).start()
            own[1, t] = send[t, TOP : TOP + MID, :]

        return carry

    lax.fori_loop(0, TILES, repack, 0)

    crow, ccol = iota((128, 512), 0), iota((128, 512), 1)
    same = (crow >> 3) == (ccol >> 5)
    shift = (ccol & 31) - (crow & 7)
    for t in range(TILES):
        comb[t] = jnp.where(jnp.logical_and(same, shift == 6 * t), 1.0, 0.0).astype(BF16)

    load_own.wait()
    load_oth.wait()
    phi[...] = jnp.zeros_like(phi)
    for s in range(2):
        both = screens[s]
        picked = jnp.where(core == 0, both[:, 0, :], both[:, 1, :])
        phi[16 * s : 16 * s + ACQ, :] = picked[0:ACQ]
        phi[16 * s + 8 : 16 * s + 8 + ACQ, :] = picked[ACQ:OWN]
    trig[0] = jnp.cos(phi[...])
    trig[1] = jnp.sin(phi[...])

    quarter = (iota((ACQ, 384), 1) >> 3) & 3

    def gram(t, buffer, cross):
        for k in range(5):
            p, q = [], []
            for b in range(2):
                v = buffer[b, t, k * GROUP : (k + 1) * GROUP, :].astype(F32)
                p.append(v[0:HALF])
                q.append(v[HALF:GROUP])
            p = jnp.concatenate(p, axis=0)
            q = jnp.concatenate(q, axis=0)
            push[0:48, 256 * k : 256 * k + 128] = p.astype(BF16)
            push[0:48, 256 * k + 128 : 256 * k + 256] = q.astype(BF16)
            push[48:96, 256 * k : 256 * k + 128] = (-q).astype(BF16)
            push[48:96, 256 * k + 128 : 256 * k + 256] = p.astype(BF16)
        raw[...] = lax.dot_general(push[...], masked[t], (((1,), (1,)), ((), ())), preferred_element_type=F32)
        for g in range(4):
            v = [raw[HALF * g + ACQ * q : HALF * g + ACQ * (q + 1), :] for q in range(QUARTERS)]
            low = jnp.where(quarter == 0, v[0], v[1])
            high = jnp.where(quarter == 2, v[2], v[3])
            red[8 * g : 8 * g + ACQ, :] = jnp.where(quarter < 2, low, high)
        stack = []
        for g in range(3):
            v = red[:, 128 * g : 128 * (g + 1)]
            hi = v.astype(BF16)
            stack += [hi, (v - hi.astype(F32)).astype(BF16)]
        out = jnp.dot(jnp.concatenate(stack, axis=0), comb[t], preferred_element_type=F32)
        for g in range(3):
            cross[g] += out[64 * g : 64 * g + 32] + out[64 * g + 32 : 64 * g + 64]

    cross1[...] = jnp.zeros_like(cross1)
    cross2[...] = jnp.zeros_like(cross2)
    red[...] = jnp.zeros_like(red)
    rim_scale = jnp.where(jnp.logical_and(core == 0, az == 0), 0.0, 1.0).astype(F32)

    def own_tile(t, carry):
        @pl.when(core == 0)
        def _():
            for b in range(2):
                arrived(t, b, 3, own, 0, RIM)
            arrived(t, 1, 4, own, RIM, TOP)

        @pl.when(core == 1)
        def _():
            arrived(t, 0, 4, own, 0, MID)

        for b in range(2):
            ownf[b, 0:RIM, :] = own[b, t, 0:RIM, :].astype(F32) * rim_scale
            ownf[b, RIM:, :] = own[b, t, RIM:, :].astype(F32)
        column = iota((8, 128), 1) + 128 * t
        mask = (((column * 3277) >> 16) - 6 * t) == iota((8, 128), 0)

        def expand(k, carry):
            for c in range(2):
                lanes = pl.ds(pl.multiple_of(256 * k + 128 * c, 128), 128)
                for a in range(OWN):
                    pieces = []
                    for q in range(QUARTERS):
                        source = k * GROUP + (HALF * c + ACQ * q + a % ACQ)
                        line = ownf[a // ACQ, pl.ds(source, 1), :]
                        pieces.append(jnp.where(mask, jnp.broadcast_to(line, (8, 128)), 0.0))
                    masked[t, 32 * a : 32 * (a + 1), lanes] = jnp.concatenate(pieces, axis=0).astype(BF16)
            return carry

        lax.fori_loop(0, 5, expand, 0)
        gram(t, own, cross1)
        return carry

    lax.fori_loop(0, TILES, own_tile, 0)

    mypow[...] = jnp.ones_like(mypow)
    for a in range(OWN):
        s = slot_of(a)
        mypow[s : s + 1, :] = cross1[a // 4, s : s + 1, 128 * (a % 4) : 128 * (a % 4 + 1)]
    pow_back = small(3, mypow, othpow, 2 * back + core)
    pow_back.start()

    tab_chip.wait_recv()

    @pl.when(core == 1)
    def _():
        for b in range(2):
            pltpu.make_async_remote_copy(
                src_ref=mytab, dst_ref=othtab.at[b], send_sem=small_send.at[1], recv_sem=small_recv.at[1 + b],
                device_id=(me, az), device_id_type=MESH,
            ).wait_recv()

    @pl.when(core == 0)
    def _():
        othtab[...] = jnp.full((2, 8, 128), -1, I32)

    slot = iota((16, 128), 0)
    real_slot = (slot & 7) < ACQ
    member = (slot >> 3) * ACQ + (slot & 7)
    own_index = jnp.where(real_slot, OWN * y + member, -9)
    oth_index = jnp.where(real_slot, OWN * (y + 1) + member, -9)
    other_table = othtab[...].reshape(16, 128)

    def weight(hit):
        return jnp.sum(jnp.where(hit, 1.0, 0.0), axis=1, keepdims=True)

    def residuals(a, cross, s, powers, w):
        k = slot_of(a)
        lanes = slice(128 * (a % 4), 128 * (a % 4 + 1))
        real = cross[a // 4, 0:16, lanes]
        imag = cross[a // 4, 16:32, lanes]
        norm = lax.rsqrt(mypow[k : k + 1, :] * powers + EPSILON) * w
        cos_a, sin_a = trig[0, k : k + 1, :], trig[1, k : k + 1, :]
        cos_b, sin_b = trig[0, 16 * s : 16 * s + 16, :], trig[1, 16 * s : 16 * s + 16, :]
        cosine = norm * (cos_a * cos_b + sin_a * sin_b)
        sine = norm * (sin_a * cos_b - cos_a * sin_b)
        return w - (real * cosine + imag * sine), imag * cosine - real * sine

    sums[...] = jnp.zeros_like(sums)
    gain = jnp.zeros((16, 128), F32)
    for a in range(OWN):
        k = slot_of(a)
        w = weight(owntab[a // ACQ, a % ACQ : a % ACQ + 1, :] == own_index)
        miss, slope = residuals(a, cross1, 0, mypow[...], w)
        gain += slope
        sums[0, k : k + 1, :] = -jnp.sum(slope, axis=0, keepdims=True)
        sums[1, k : k + 1, :] = jnp.sum(miss, axis=0, keepdims=True)
    sums[0] += gain

    pow_back.wait_recv()

    def other_tile(t, carry):
        @pl.when(core == 0)
        def _():
            for b in range(2):
                arrived(t, b, 2, oth, 0, RIM)
                arrived(t, b, 0, oth, RIM, TOP)

        @pl.when(core == 1)
        def _():
            for b in range(2):
                arrived(t, b, 1, oth, 0, MID)

        gram(t, oth, cross2)
        return carry

    lax.fori_loop(0, TILES, other_tile, 0)

    first = jnp.where(core == 0, 1.0, 0.0).astype(F32)
    gain = jnp.zeros((16, 128), F32)
    loss = jnp.zeros((16, 128), F32)
    for a in range(OWN):
        k = slot_of(a)
        mine = owntab[a // ACQ, a % ACQ : a % ACQ + 1, :] == oth_index
        theirs = other_table == OWN * y + a
        w = weight(jnp.where(core == 0, mine.astype(I32), theirs.astype(I32)) > 0)
        miss, slope = residuals(a, cross2, 1, othpow[...], w)
        gain += slope
        loss += miss
        sums[0, k : k + 1, :] += -jnp.sum(slope, axis=0, keepdims=True)
        sums[1, k : k + 1, :] += first * jnp.sum(miss, axis=0, keepdims=True)
    for b in range(2):
        for f in range(2):
            msg_own[b, 8 * f : 8 * f + 8, :] = sums[f, 8 * b : 8 * b + 8, :]
        msg_oth[b, 0:8, :] = gain[8 * b : 8 * b + 8]
        msg_oth[b, 8:16, :] = (1.0 - first) * loss[8 * b : 8 * b + 8]
    fin_chip = small(4, msg_own.at[1 - core], fin_own.at[core], 2 * y + 1 - core)
    fin_chip.start()

    def fin_side(b):
        return pltpu.make_async_remote_copy(
            src_ref=msg_oth.at[b], dst_ref=fin_oth.at[core], send_sem=small_send.at[5 + b],
            recv_sem=small_recv.at[5 + core], device_id=(2 * side + b, az), device_id_type=MESH,
        )

    for b in range(2):
        fin_side(b).start()
    fin_own[core] = msg_own[core]
    fin_chip.wait_recv()
    for c in range(2):
        pltpu.make_async_remote_copy(
            src_ref=msg_oth.at[c], dst_ref=fin_oth.at[c], send_sem=small_send.at[5 + c],
            recv_sem=small_recv.at[5 + c], device_id=(me, az), device_id_type=MESH,
        ).wait_recv()
    for j in range(2):
        total = fin_own[j] + fin_oth[j]
        grad_ref[:, j, :] = total[0:ACQ]
        misfit_ref[:, j, :] = total[8 : 8 + ACQ]

    def drain(t, carry):
        for copy in wide_copies(t):
            copy.wait_send()

        @pl.when(core == 0)
        def _():
            chip_copy0(t).wait_send()

        @pl.when(core == 1)
        def _():
            chip_copy1(t).wait_send()

        return carry

    lax.fori_loop(0, TILES, drain, 0)
    tab_chip.wait_send()
    tab_up().wait_send()
    pow_back.wait_send()
    fin_chip.wait_send()
    for b in range(2):
        fin_side(b).wait_send()


def local(chips, slabs, complex_slabs, secondaries, pair_counts, phase_screens):
    rows, columns = complex_slabs.shape[2:]
    x = complex_slabs.reshape(2 * ACQ, rows, columns)
    vmem = pl.BlockSpec(memory_space=pltpu.VMEM)
    hbm = pl.BlockSpec(memory_space=pl.ANY)
    out = jax.ShapeDtypeStruct((ACQ, 2, 128), F32)
    return pl.pallas_call(
        functools.partial(kernel, chips, slabs),
        out_shape=(out, out),
        in_specs=[hbm, vmem, pl.BlockSpec(memory_space=pltpu.SMEM), hbm],
        out_specs=(vmem, vmem),
        scratch_shapes=[
            pltpu.VMEM((2 * ACQ, rows, columns), BF16),
            pltpu.VMEM((2, OWN, 2, 128), F32),
            pltpu.VMEM((10 * GROUP, 2 * ACQ * 16 * QUARTERS), BF16),
            pltpu.VMEM((TILES, 10 * GROUP, 128), BF16),
            pltpu.VMEM((2, TILES, 5 * GROUP, 128), BF16),
            pltpu.VMEM((2, TILES, 5 * GROUP, 128), BF16),
            pltpu.VMEM((2, 5 * GROUP, 128), F32),
            pltpu.VMEM((TILES, 32 * OWN, 1280), BF16),
            pltpu.VMEM((96, 1280), BF16),
            pltpu.VMEM((96, 32 * OWN), F32),
            pltpu.VMEM((32, 32 * OWN), F32),
            pltpu.VMEM((TILES, 128, 512), BF16),
            pltpu.VMEM((3, 32, 512), F32),
            pltpu.VMEM((3, 32, 512), F32),
            pltpu.VMEM((8, 128), I32),
            pltpu.VMEM((2, 8, 128), I32),
            pltpu.VMEM((2, 8, 128), I32),
            pltpu.VMEM((16, 128), F32),
            pltpu.VMEM((16, 128), F32),
            pltpu.VMEM((32, 128), F32),
            pltpu.VMEM((2, 32, 128), F32),
            pltpu.VMEM((2, 16, 128), F32),
            pltpu.VMEM((2, 16, 128), F32),
            pltpu.VMEM((2, 16, 128), F32),
            pltpu.VMEM((2, 16, 128), F32),
            pltpu.VMEM((2, 16, 128), F32),
            pltpu.SemaphoreType.DMA((3,)),
            pltpu.SemaphoreType.DMA((TILES, 5)),
            pltpu.SemaphoreType.DMA((TILES, 2, 5)),
            pltpu.SemaphoreType.DMA((7,)),
            pltpu.SemaphoreType.DMA((7,)),
        ],
        compiler_params=pltpu.CompilerParams(
            collective_id=0, has_side_effects=True, vmem_limit_bytes=40 * 1024 * 1024
        ),
    )(x, secondaries, pair_counts, phase_screens)


def solution(mesh):
    return jax.shard_map(
        functools.partial(local, mesh.shape["acq"] // 2, mesh.shape["az"]),
        mesh=mesh,
        in_specs=(P("acq", None, "az", None), P("acq", None), P("acq"), P(None, "az", None)),
        out_specs=(P("acq", "az", None), P("acq", "az", None)),
        check_vma=False,
    )
```

```python
import functools

import jax
import jax.numpy as jnp
import numpy as np
from jax import lax
from jax.experimental import pallas as pl
from jax.experimental.pallas import tpu as pltpu
from jax.sharding import PartitionSpec as P

EPSILON = 1e-6
MESH = pl.DeviceIdType.MESH
F32, BF16, I32 = jnp.float32, jnp.bfloat16, jnp.int32

ACQ = 6
OWN = 12
QUARTERS = 4
TILES = 5
GROUP = 2 * QUARTERS * ACQ
HALF = QUARTERS * ACQ
TOP, MID, RIM = 3 * GROUP, 5 * GROUP, 2 * GROUP


WIDE = TILES * 128


def gather_matrix():
    row, col = np.arange(WIDE)[:, None], np.arange(512)[None, :]
    tile, lane = row // 128, row % 128
    combine = np.logical_and(lane // 8 == col // 32, 6 * tile + lane % 8 == col % 32)
    sums = row // 20 == np.arange(128)[None, :] % 32
    return jnp.asarray(np.concatenate([combine, sums], axis=1), BF16)


def slot_of(a):
    return a // ACQ * 8 + a % ACQ


def iota(shape, dim):
    return lax.broadcasted_iota(I32, shape, dim)


def kernel(
    chips, slabs,
    x_hbm, sec_hbm, cnt_hbm, screens_hbm, gather_hbm,
    grad_ref, misfit_ref,
    xbuf, secs, cnts, screens, gather, spread, send, own, oth, ownf, masked, acc, raw, red, cross, power,
    mytab, owntab, othtab, mypow, othpow, phi, trig, turn, sums, msg_own, msg_oth, fin_own, fin_oth,
    load_sem, send_sem, rim_send, oth_recv, own_recv, rim_recv, small_send, small_recv,
):
    me = lax.axis_index("acq")
    az = lax.axis_index("az")
    y, core = me // 2, me % 2
    up, down = jnp.minimum(y + 1, chips - 1), jnp.maximum(y - 1, 0)
    az_next, az_prev = jnp.minimum(az + 1, slabs - 1), jnp.maximum(az - 1, 0)
    has_up, has_down = y < chips - 1, y > 0
    has_next, has_prev = az < slabs - 1, az > 0
    side = jnp.where(core == 0, up, down)
    has_side = jnp.logical_or(jnp.logical_and(core == 0, has_up), jnp.logical_and(core == 1, has_down))
    has_rim = jnp.logical_and(core == 0, has_prev)
    both = jnp.logical_and

    loads = [pltpu.make_async_copy(x_hbm.at[pl.ds(3 * i, 3)], xbuf.at[pl.ds(3 * i, 3)], load_sem.at[i]) for i in range(4)]
    loads += [
        pltpu.make_async_copy(sec_hbm, secs, load_sem.at[4]),
        pltpu.make_async_copy(cnt_hbm, cnts, load_sem.at[5]),
        pltpu.make_async_copy(screens_hbm.at[pl.ds(OWN * y, OWN)], screens.at[0], load_sem.at[6]),
        pltpu.make_async_copy(screens_hbm.at[pl.ds(OWN * side, OWN)], screens.at[1], load_sem.at[7]),
        pltpu.make_async_copy(gather_hbm, gather, load_sem.at[8]),
    ]
    for load in loads:
        load.start()

    fin_oth[...] = jnp.zeros_like(fin_oth)
    othtab[...] = jnp.full((2, 8, 128), -1, I32)

    barrier = pltpu.get_barrier_semaphore()

    def greet(a, z):
        pl.semaphore_signal(barrier, inc=1, device_id=(a, z), device_id_type=MESH)

    greet(2 * y + 1 - core, az)

    @pl.when(has_up)
    def _():
        for c in range(2):
            greet(2 * up + c, az)

    @pl.when(has_down)
    def _():
        for c in range(2):
            greet(2 * down + c, az)

    @pl.when(has_rim)
    def _():
        for c in range(2):
            greet(2 * y + c, az_prev)

        @pl.when(has_up)
        def _():
            for c in range(2):
                greet(2 * up + c, az_prev)

    def flag(condition):
        return jnp.where(condition, 1, 0)

    expected = 1 + 2 * flag(has_up) + 2 * flag(has_down) + flag(has_next) + flag(both(has_next, has_down))

    @pl.when(both(core == 0, jnp.logical_not(has_prev)))
    def _():
        own[:, :, 0:RIM, :] = jnp.zeros((2, TILES, RIM, 128), BF16)
        oth[:, :, 0:RIM, :] = jnp.zeros((2, TILES, RIM, 128), BF16)

    @pl.when(jnp.logical_not(has_side))
    def _():
        oth[...] = jnp.zeros_like(oth)

    loads[4].wait()
    loads[5].wait()
    mytab[...] = jnp.full((8, 128), -1, I32)
    mytab[0:ACQ, 0:10] = secs[...]
    slots = jnp.zeros((8, 128), I32)
    for i in range(ACQ):
        slots = jnp.where(iota((8, 128), 0) == i, cnts[i], slots)
    mytab[...] = jnp.where(iota((8, 128), 1) < slots, mytab[...], -1)
    owntab[core] = mytab[...]

    def small(k, src, dst, a, sem):
        return pltpu.make_async_remote_copy(
            src_ref=src, dst_ref=dst, send_sem=small_send.at[k], recv_sem=small_recv.at[sem],
            device_id=(a, az), device_id_type=MESH,
        )

    def wide(t, k, first, rows, buffer, start, a, sem):
        return pltpu.make_async_remote_copy(
            src_ref=send.at[t, pl.ds(first, rows)],
            dst_ref=buffer.at[core, t, pl.ds(start, rows)],
            send_sem=send_sem.at[t, k], recv_sem=sem,
            device_id=(a, az), device_id_type=MESH,
        )

    def to_down(t):
        return wide(t, 0, 0, TOP, oth, RIM, 2 * down, oth_recv.at[t, core])

    def to_up(t):
        return wide(t, 1, TOP, MID, oth, 0, 2 * up + 1, oth_recv.at[t, core])

    def to_core1(t):
        return wide(t, 2, TOP, MID, own, 0, 2 * y + 1, own_recv.at[t])

    def to_core0(t):
        return wide(t, 2, 0, TOP, own, RIM, 2 * y, own_recv.at[t])

    def rim_copy(k, buffer, a):
        return pltpu.make_async_remote_copy(
            src_ref=send.at[:, pl.ds(TOP + MID, RIM)],
            dst_ref=buffer.at[core, :, pl.ds(0, RIM)],
            send_sem=rim_send.at[k], recv_sem=rim_recv.at[k, core],
            device_id=(a, az_next), device_id_type=MESH,
        )

    def unpack(t, first, rows):
        for q in range(QUARTERS):
            lanes = pl.ds(pl.multiple_of(640 * q + 128 * t, 128), 128)
            for ac in range(2 * ACQ):
                start = (q * 2 * ACQ + ac) * 16 + first
                spread[start : start + rows, :] = xbuf[ac, first : first + rows, lanes].astype(F32)

    def pick(t, first, last):
        for r in range(first, last):
            parts = [spread[pl.ds(16 * c + r, HALF, stride=32), :] for c in range(2)]
            send[t, r * GROUP : (r + 1) * GROUP, :] = jnp.concatenate(parts, axis=0).astype(BF16)

    for i in range(4):
        loads[i].wait()

    def rim_tile(t, carry):
        unpack(t, 8, 2)
        pick(t, 8, 10)
        return carry

    lax.fori_loop(0, TILES, rim_tile, 0)
    pl.semaphore_wait(barrier, expected)

    @pl.when(has_next)
    def _():
        rim_copy(0, own, 2 * y).start()

        @pl.when(has_down)
        def _():
            rim_copy(1, oth, 2 * down).start()

    def main_tile(t, carry):
        unpack(t, 0, 8)
        pick(t, 0, 8)

        @pl.when(has_down)
        def _():
            to_down(t).start()

        @pl.when(has_up)
        def _():
            to_up(t).start()

        @pl.when(core == 0)
        def _():
            to_core1(t).start()
            own[0, t, RIM:, :] = send[t, 0:TOP, :]

        @pl.when(core == 1)
        def _():
            to_core0(t).start()
            own[1, t] = send[t, TOP : TOP + MID, :]

        return carry

    lax.fori_loop(0, TILES, main_tile, 0)

    tab_chip = small(0, mytab, owntab.at[core], 2 * y + 1 - core, 0)
    tab_chip.start()

    def tab_up(c):
        return small(1, mytab, othtab.at[c], 2 * up + 1, 1 + c)

    @pl.when(has_up)
    def _():
        tab_up(core).start()

    quarter = (iota((ACQ, 384), 1) >> 3) & 3

    def expand(t, first, last):
        column = iota((16, 128), 1) + 128 * t
        mask = jnp.where((((column * 3277) >> 16) - 6 * t) == (iota((16, 128), 0) & 7), 1.0, 0.0).astype(BF16)

        def step(k, carry):
            lanes = pl.ds(pl.multiple_of(128 * k, 128), 128)
            for c in range(2):
                for a in range(OWN):
                    for q in range(0, QUARTERS, 2):
                        source = k * GROUP + (HALF * c + ACQ * q + a % ACQ)
                        low = jnp.broadcast_to(ownf[a // ACQ, pl.ds(source, 1), :], (8, 128))
                        high = jnp.broadcast_to(ownf[a // ACQ, pl.ds(source + ACQ, 1), :], (8, 128))
                        start = 384 * c + 32 * a + 8 * q
                        masked[t, start : start + 16, lanes] = jnp.concatenate([low, high], axis=0).astype(BF16) * mask
            return carry

        lax.fori_loop(first, last, step, 0)

    def products(t, buffer, first, last):
        blocks = []
        for b in range(2):
            rows = [buffer[b, t, k * GROUP : (k + 1) * GROUP, :] for k in range(first, last)]
            blocks.append(jnp.concatenate(rows, axis=1))
        out = lax.dot_general(
            jnp.concatenate(blocks, axis=0), masked[t, :, 128 * first : 128 * last],
            (((1,), (1,)), ((), ())), preferred_element_type=F32,
        )
        real, imag = [], []
        for b in range(2):
            p, q = out[GROUP * b : GROUP * b + HALF], out[GROUP * b + HALF : GROUP * (b + 1)]
            real.append(p[:, :384] + q[:, 384:])
            imag.append(p[:, 384:] - q[:, :384])
        return jnp.concatenate(real + imag, axis=0)

    def squares(t, first, last):
        parts = []
        for b in range(2):
            total = None
            for k in range(first, last):
                v = oth[b, t, k * GROUP : (k + 1) * GROUP, :].astype(F32)
                term = v[:HALF] * v[:HALF] + v[HALF:] * v[HALF:]
                total = term if total is None else total + term
            parts.append(total)
        return jnp.concatenate(parts, axis=0)

    def own_tile(t, carry):
        @pl.when(core == 0)
        def _():
            to_core0(t).wait_recv()

        @pl.when(core == 1)
        def _():
            to_core1(t).wait_recv()

        for b in range(2):
            ownf[b, RIM:, :] = own[b, t, RIM:, :].astype(F32)
        expand(t, 2, 5)
        acc[0, t] = products(t, own, 2, 5)
        return carry

    lax.fori_loop(0, TILES, own_tile, 0)

    loads[6].wait()
    loads[7].wait()
    phi[...] = jnp.zeros_like(phi)
    for s in range(2):
        rows = screens[s]
        picked = jnp.where(core == 0, rows[:, 0, :], rows[:, 1, :])
        phi[16 * s : 16 * s + ACQ, :] = picked[0:ACQ]
        phi[16 * s + 8 : 16 * s + 8 + ACQ, :] = picked[ACQ:OWN]
    trig[0] = jnp.cos(phi[...])
    trig[1] = jnp.sin(phi[...])

    tab_chip.wait_recv()

    @pl.when(both(core == 1, has_down))
    def _():
        for c in range(2):
            tab_up(c).wait_recv()

    slot = iota((16, 128), 0)
    real_slot = (slot & 7) < ACQ
    member = (slot >> 3) * ACQ + (slot & 7)
    own_index = jnp.where(real_slot, OWN * y + member, -9)
    oth_index = jnp.where(real_slot, OWN * (y + 1) + member, -9)
    other_table = othtab[...].reshape(16, 128)
    for a in range(OWN):
        k = slot_of(a)
        cos_a, sin_a = trig[0, k : k + 1, :], trig[1, k : k + 1, :]
        line = owntab[a // ACQ, a % ACQ : a % ACQ + 1, :]
        theirs = jnp.where(other_table == OWN * y + a, 1.0, 0.0)
        hits = (
            jnp.where(line == own_index, 1.0, 0.0),
            jnp.where(core == 0, jnp.where(line == oth_index, 1.0, 0.0), theirs),
        )
        for s in range(2):
            w = jnp.sum(hits[s], axis=1, keepdims=True)
            cos_b, sin_b = trig[0, 16 * s : 16 * s + 16, :], trig[1, 16 * s : 16 * s + 16, :]
            turn[s, a, 0] = w * (cos_a * cos_b + sin_a * sin_b)
            turn[s, a, 1] = w * (sin_a * cos_b - cos_a * sin_b)
            turn[s, a, 2] = jnp.broadcast_to(w, (16, 128))

    def other_tile(t, carry):
        @pl.when(both(core == 0, has_up))
        def _():
            for b in range(2):
                wide(t, 0, 0, TOP, oth, RIM, me, oth_recv.at[t, b]).wait_recv()

        @pl.when(both(core == 1, has_down))
        def _():
            for b in range(2):
                wide(t, 1, TOP, MID, oth, 0, me, oth_recv.at[t, b]).wait_recv()

        acc[1, t] = products(t, oth, 2, 5)
        power[t] = squares(t, 2, 5)
        return carry

    lax.fori_loop(0, TILES, other_tile, 0)

    @pl.when(has_rim)
    def _():
        for b in range(2):
            pltpu.make_async_remote_copy(
                src_ref=send.at[:, pl.ds(TOP + MID, RIM)], dst_ref=own.at[b, :, pl.ds(0, RIM)],
                send_sem=rim_send.at[0], recv_sem=rim_recv.at[0, b], device_id=(me, az), device_id_type=MESH,
            ).wait_recv()

        @pl.when(has_up)
        def _():
            for b in range(2):
                pltpu.make_async_remote_copy(
                    src_ref=send.at[:, pl.ds(TOP + MID, RIM)], dst_ref=oth.at[b, :, pl.ds(0, RIM)],
                    send_sem=rim_send.at[1], recv_sem=rim_recv.at[1, b], device_id=(me, az), device_id_type=MESH,
                ).wait_recv()

    red[...] = jnp.zeros_like(red)

    def rim_rows(t, carry):
        for b in range(2):
            ownf[b, 0:RIM, :] = own[b, t, 0:RIM, :].astype(F32)
        expand(t, 0, 2)
        for s, buffer in enumerate((own, oth)):
            raw[s] = products(t, buffer, 0, 2) + acc[s, t]
            for g in range(4):
                v = [raw[s, HALF * g + ACQ * q : HALF * g + ACQ * (q + 1), :] for q in range(QUARTERS)]
                low = jnp.where(quarter == 0, v[0], v[1])
                high = jnp.where(quarter == 2, v[2], v[3])
                red[s, t, 8 * g : 8 * g + ACQ, :] = jnp.where(quarter < 2, low, high)
        power[t] += squares(t, 0, 2)
        return carry

    lax.fori_loop(0, TILES, rim_rows, 0)

    def split(v):
        high = v.astype(BF16)
        return [high, (v - high.astype(F32)).astype(BF16)]

    loads[8].wait()
    summed = jnp.concatenate(split(jnp.concatenate([power[t] for t in range(TILES)], axis=1)), axis=0)
    summed = jnp.dot(summed, gather[:, 512:], preferred_element_type=F32)
    power[0] = summed[0:48] + summed[48:96]
    othpow[...] = jnp.ones_like(othpow)
    cell_quarter = iota((ACQ, 128), 1) >> 5
    for b in range(2):
        v = [power[0, HALF * b + ACQ * q : HALF * b + ACQ * (q + 1), :] for q in range(QUARTERS)]
        low = jnp.where(cell_quarter == 0, v[0], v[1])
        high = jnp.where(cell_quarter == 2, v[2], v[3])
        othpow[8 * b : 8 * b + ACQ, :] = jnp.where(cell_quarter < 2, low, high)

    for s in range(2):
        stack = []
        for g in range(3):
            stack += split(jnp.concatenate([red[s, t, :, 128 * g : 128 * (g + 1)] for t in range(TILES)], axis=1))
        out = jnp.dot(jnp.concatenate(stack, axis=0), gather[:, :512], preferred_element_type=F32)
        for g in range(3):
            cross[s, g] = out[64 * g : 64 * g + 32] + out[64 * g + 32 : 64 * g + 64]

    mypow[...] = jnp.ones_like(mypow)
    for a in range(OWN):
        k = slot_of(a)
        mypow[k : k + 1, :] = cross[0, a // 4, k : k + 1, 128 * (a % 4) : 128 * (a % 4 + 1)]

    first = jnp.where(core == 0, 1.0, 0.0).astype(F32)
    sums[...] = jnp.zeros_like(sums)
    gain = [jnp.zeros((16, 128), F32), jnp.zeros((16, 128), F32)]
    loss = jnp.zeros((16, 128), F32)
    for a in range(OWN):
        k = slot_of(a)
        slopes, misses = [], []
        for s, powers in enumerate((mypow[...], othpow[...])):
            lanes = slice(128 * (a % 4), 128 * (a % 4 + 1))
            real, imag = cross[s, a // 4, 0:16, lanes], cross[s, a // 4, 16:32, lanes]
            norm = lax.rsqrt(mypow[k : k + 1, :] * powers + EPSILON)
            cosine, sine = turn[s, a, 0], turn[s, a, 1]
            slope = norm * (imag * cosine - real * sine)
            gain[s] += slope
            slopes.append(slope)
            misses.append(turn[s, a, 2] - norm * (real * cosine + imag * sine))
        loss += misses[1]
        sums[0, k : k + 1, :] = -jnp.sum(slopes[0] + slopes[1], axis=0, keepdims=True)
        sums[1, k : k + 1, :] = jnp.sum(misses[0] + first * misses[1], axis=0, keepdims=True)
    sums[0] += gain[0]
    for b in range(2):
        for f in range(2):
            msg_own[b, 8 * f : 8 * f + 8, :] = sums[f, 8 * b : 8 * b + 8, :]
        msg_oth[b, 0:8, :] = gain[1][8 * b : 8 * b + 8]
        msg_oth[b, 8:16, :] = (1.0 - first) * loss[8 * b : 8 * b + 8]
    fin_chip = small(2, msg_own.at[1 - core], fin_own.at[core], 2 * y + 1 - core, 3)
    fin_chip.start()

    def fin_side(b):
        return small(3 + b, msg_oth.at[b], fin_oth.at[core], 2 * side + b, 4 + core)

    @pl.when(has_side)
    def _():
        for b in range(2):
            fin_side(b).start()

    fin_own[core] = msg_own[core]
    fin_chip.wait_recv()

    @pl.when(has_down)
    def _():
        small(3, msg_oth.at[0], fin_oth.at[0], me, 4).wait_recv()

    @pl.when(has_up)
    def _():
        small(3, msg_oth.at[1], fin_oth.at[1], me, 5).wait_recv()

    for j in range(2):
        total = fin_own[j] + fin_oth[j]
        grad_ref[:, j, :] = total[0:ACQ]
        misfit_ref[:, j, :] = total[8 : 8 + ACQ]

    def drain(t, carry):
        @pl.when(has_down)
        def _():
            to_down(t).wait_send()

        @pl.when(has_up)
        def _():
            to_up(t).wait_send()

        @pl.when(core == 0)
        def _():
            to_core1(t).wait_send()

        @pl.when(core == 1)
        def _():
            to_core0(t).wait_send()

        return carry

    lax.fori_loop(0, TILES, drain, 0)

    @pl.when(has_next)
    def _():
        rim_copy(0, own, 2 * y).wait_send()

        @pl.when(has_down)
        def _():
            rim_copy(1, oth, 2 * down).wait_send()

    tab_chip.wait_send()

    @pl.when(has_up)
    def _():
        tab_up(core).wait_send()

    fin_chip.wait_send()

    @pl.when(has_side)
    def _():
        for b in range(2):
            fin_side(b).wait_send()


def local(chips, slabs, complex_slabs, secondaries, pair_counts, phase_screens):
    rows, columns = complex_slabs.shape[2:]
    x = complex_slabs.reshape(2 * ACQ, rows, columns)
    vmem = pl.BlockSpec(memory_space=pltpu.VMEM)
    hbm = pl.BlockSpec(memory_space=pltpu.HBM)
    out = jax.ShapeDtypeStruct((ACQ, 2, 128), F32)
    return pl.pallas_call(
        functools.partial(kernel, chips, slabs),
        out_shape=(out, out),
        in_specs=[hbm] * 5,
        out_specs=(vmem, vmem),
        scratch_shapes=[
            pltpu.VMEM((2 * ACQ, rows, columns), BF16),
            pltpu.VMEM(secondaries.shape, I32),
            pltpu.SMEM(pair_counts.shape, I32),
            pltpu.VMEM((2, OWN, 2, 128), F32),
            pltpu.VMEM((WIDE, 640), BF16),
            pltpu.VMEM((2 * ACQ * QUARTERS * 16, 128), F32),
            pltpu.VMEM((TILES, 10 * GROUP, 128), BF16),
            pltpu.VMEM((2, TILES, 5 * GROUP, 128), BF16),
            pltpu.VMEM((2, TILES, 5 * GROUP, 128), BF16),
            pltpu.VMEM((2, 5 * GROUP, 128), F32),
            pltpu.VMEM((TILES, 64 * OWN, WIDE), BF16),
            pltpu.VMEM((2, TILES, 96, 32 * OWN), F32),
            pltpu.VMEM((2, 96, 32 * OWN), F32),
            pltpu.VMEM((2, TILES, 32, 32 * OWN), F32),
            pltpu.VMEM((2, 3, 32, 512), F32),
            pltpu.VMEM((TILES, 48, 128), F32),
            pltpu.VMEM((8, 128), I32),
            pltpu.VMEM((2, 8, 128), I32),
            pltpu.VMEM((2, 8, 128), I32),
            pltpu.VMEM((16, 128), F32),
            pltpu.VMEM((16, 128), F32),
            pltpu.VMEM((32, 128), F32),
            pltpu.VMEM((2, 32, 128), F32),
            pltpu.VMEM((2, OWN, 3, 16, 128), F32),
            pltpu.VMEM((2, 16, 128), F32),
            pltpu.VMEM((2, 16, 128), F32),
            pltpu.VMEM((2, 16, 128), F32),
            pltpu.VMEM((2, 16, 128), F32),
            pltpu.VMEM((2, 16, 128), F32),
            pltpu.SemaphoreType.DMA((9,)),
            pltpu.SemaphoreType.DMA((TILES, 3)),
            pltpu.SemaphoreType.DMA((2,)),
            pltpu.SemaphoreType.DMA((TILES, 2)),
            pltpu.SemaphoreType.DMA((TILES,)),
            pltpu.SemaphoreType.DMA((2, 2)),
            pltpu.SemaphoreType.DMA((5,)),
            pltpu.SemaphoreType.DMA((6,)),
        ],
        compiler_params=pltpu.CompilerParams(
            collective_id=0, has_side_effects=True, vmem_limit_bytes=40 * 1024 * 1024
        ),
    )(x, secondaries, pair_counts, phase_screens, gather_matrix())


def solution(mesh):
    return jax.shard_map(
        functools.partial(local, mesh.shape["acq"] // 2, mesh.shape["az"]),
        mesh=mesh,
        in_specs=(P("acq", None, "az", None), P("acq", None), P("acq"), P(None, "az", None)),
        out_specs=(P("acq", "az", None), P("acq", "az", None)),
        check_vma=False,
    )
```

```python
import functools

import jax
import jax.numpy as jnp
from jax import lax
from jax.experimental import pallas as pl
from jax.experimental.pallas import tpu as pltpu
from jax.sharding import PartitionSpec as P

EPSILON = 1e-6
MESH = pl.DeviceIdType.MESH
F32, BF16, I32 = jnp.float32, jnp.bfloat16, jnp.int32

ACQ = 6
OWN = 12
QUARTERS, TILES, QUARTER = 4, 5, 640
TOP, MID, RIM = 3, 5, 2


def iota(shape, dim):
    return lax.broadcasted_iota(I32, shape, dim)


def kernel(
    chips, slabs,
    x_hbm, sec_hbm, cnt_hbm, screens_hbm,
    grad_ref, misfit_ref,
    secs, cnts, screens, own, oth, ownf, othf, masked, acc, turned, square, power,
    mytab, owntab, othtab, partners, mypow, othpow, phi, trig, turn, sums, other_sums, msg_own, msg_oth, fin_own, fin_oth,
    load_sem, local_sem, send_sem, rim_send, oth_recv, own_recv, rim_recv, small_send, small_recv,
):
    me = lax.axis_index("acq")
    az = lax.axis_index("az")
    y, core = me // 2, me % 2
    up, down = jnp.minimum(y + 1, chips - 1), jnp.maximum(y - 1, 0)
    az_next, az_prev = jnp.minimum(az + 1, slabs - 1), jnp.maximum(az - 1, 0)
    has_up, has_down = y < chips - 1, y > 0
    has_next, has_prev = az < slabs - 1, az > 0
    side = jnp.where(core == 0, up, down)
    has_side = jnp.logical_or(jnp.logical_and(core == 0, has_up), jnp.logical_and(core == 1, has_down))
    has_rim = jnp.logical_and(core == 0, has_prev)
    both = jnp.logical_and

    loads = [
        pltpu.make_async_copy(sec_hbm, secs, load_sem.at[0]),
        pltpu.make_async_copy(cnt_hbm, cnts, load_sem.at[1]),
        pltpu.make_async_copy(screens_hbm.at[pl.ds(OWN * y, OWN)], screens.at[0], load_sem.at[2]),
        pltpu.make_async_copy(screens_hbm.at[pl.ds(OWN * side, OWN)], screens.at[1], load_sem.at[3]),
    ]
    for load in loads:
        load.start()

    def columns(q):
        return pl.ds(pl.multiple_of(QUARTER * q, 128), QUARTER)

    def local_top(q):
        return pltpu.make_async_copy(
            x_hbm.at[:, pl.ds(0, TOP), :, columns(q)], own.at[0, :, pl.ds(RIM, TOP), :, columns(q)], local_sem.at[q]
        )

    def local_mid(q):
        return pltpu.make_async_copy(
            x_hbm.at[:, pl.ds(TOP, MID), :, columns(q)], own.at[1, :, :, :, columns(q)], local_sem.at[q]
        )

    @pl.when(core == 0)
    def _():
        for q in range(QUARTERS):
            local_top(q).start()

    @pl.when(core == 1)
    def _():
        for q in range(QUARTERS):
            local_mid(q).start()

    fin_oth[...] = jnp.zeros_like(fin_oth)
    msg_own[...] = jnp.zeros_like(msg_own)
    msg_oth[...] = jnp.zeros_like(msg_oth)
    othtab[...] = jnp.full((2, 8, 128), -1, I32)

    barrier = pltpu.get_barrier_semaphore()

    def greet(a, z):
        pl.semaphore_signal(barrier, inc=1, device_id=(a, z), device_id_type=MESH)

    greet(2 * y + 1 - core, az)

    @pl.when(has_up)
    def _():
        for c in range(2):
            greet(2 * up + c, az)

    @pl.when(has_down)
    def _():
        for c in range(2):
            greet(2 * down + c, az)

    @pl.when(has_rim)
    def _():
        for c in range(2):
            greet(2 * y + c, az_prev)

        @pl.when(has_up)
        def _():
            for c in range(2):
                greet(2 * up + c, az_prev)

    def flag(condition):
        return jnp.where(condition, 1, 0)

    expected = 1 + 2 * flag(has_up) + 2 * flag(has_down) + flag(has_next) + flag(both(has_next, has_down))

    @pl.when(both(core == 0, jnp.logical_not(has_prev)))
    def _():
        own[:, :, 0:RIM] = jnp.zeros((2, ACQ, RIM, 2, QUARTERS * QUARTER), BF16)
        oth[:, :, 0:RIM] = jnp.zeros((2, ACQ, RIM, 2, QUARTERS * QUARTER), BF16)

    @pl.when(jnp.logical_not(has_side))
    def _():
        oth[...] = jnp.zeros_like(oth)

    loads[0].wait()
    loads[1].wait()
    mytab[...] = jnp.full((8, 128), -1, I32)
    mytab[0:ACQ, 0:10] = secs[...]
    slots = jnp.zeros((8, 128), I32)
    for i in range(ACQ):
        slots = jnp.where(iota((8, 128), 0) == i, cnts[i], slots)
    mytab[...] = jnp.where(iota((8, 128), 1) < slots, mytab[...], -1)
    owntab[core] = mytab[...]

    def small(k, src, dst, a, sem):
        return pltpu.make_async_remote_copy(
            src_ref=src, dst_ref=dst, send_sem=small_send.at[k], recv_sem=small_recv.at[sem],
            device_id=(a, az), device_id_type=MESH,
        )

    def wide(q, k, first, rows, buffer, start, a, sem):
        return pltpu.make_async_remote_copy(
            src_ref=x_hbm.at[:, pl.ds(first, rows), :, columns(q)],
            dst_ref=buffer.at[core, :, pl.ds(start, rows), :, columns(q)],
            send_sem=send_sem.at[q, k], recv_sem=sem,
            device_id=(a, az), device_id_type=MESH,
        )

    def to_down(q):
        return wide(q, 0, 0, TOP, oth, RIM, 2 * down, oth_recv.at[q, core])

    def to_up(q):
        return wide(q, 1, TOP, MID, oth, 0, 2 * up + 1, oth_recv.at[q, core])

    def to_core1(q):
        return wide(q, 2, TOP, MID, own, 0, 2 * y + 1, own_recv.at[q])

    def to_core0(q):
        return wide(q, 2, 0, TOP, own, RIM, 2 * y, own_recv.at[q])

    def rim_copy(k, block, buffer, a, z):
        return pltpu.make_async_remote_copy(
            src_ref=x_hbm.at[:, pl.ds(TOP + MID, RIM)],
            dst_ref=buffer.at[block, :, pl.ds(0, RIM)],
            send_sem=rim_send.at[k], recv_sem=rim_recv.at[k, block],
            device_id=(a, z), device_id_type=MESH,
        )

    pl.semaphore_wait(barrier, expected)

    @pl.when(has_next)
    def _():
        rim_copy(0, core, own, 2 * y, az_next).start()

        @pl.when(has_down)
        def _():
            rim_copy(1, core, oth, 2 * down, az_next).start()

    def start_wide(q, carry):
        @pl.when(core == 0)
        def _():
            to_core1(q).start()

        @pl.when(core == 1)
        def _():
            to_core0(q).start()

        @pl.when(has_down)
        def _():
            to_down(q).start()

        @pl.when(has_up)
        def _():
            to_up(q).start()

        return carry

    lax.fori_loop(0, QUARTERS, start_wide, 0)

    tab_chip = small(0, mytab, owntab.at[core], 2 * y + 1 - core, 0)
    tab_chip.start()

    def tab_up(c):
        return small(1, mytab, othtab.at[c], 2 * up + 1, 1 + c)

    @pl.when(has_up)
    def _():
        tab_up(core).start()

    def lay(buffer, rows, q, first, last):
        for r in range(first, last):
            for a in range(OWN):
                v = buffer[a // ACQ, a % ACQ, r, :, columns(q)].astype(F32)
                for t in range(TILES):
                    rows[r, q, pl.ds(2 * OWN * t + a, 2, stride=OWN), :] = v[:, 128 * t : 128 * (t + 1)]

    def cell_mask(t):
        column = iota((16, 128), 1) + 128 * t
        slot = ((column * 3277) >> 16) - 6 * t
        return jnp.where(slot == (iota((16, 128), 0) & 7), 1.0, 0.0).astype(BF16)

    masks = [cell_mask(t) for t in range(TILES)]

    def expand(q, t, first, last):
        for r in range(first, last):
            for c in range(2):
                start = 256 * r + 128 * c
                for a in range(0, OWN, 2):
                    source = 2 * OWN * t + OWN * c + a
                    low = jnp.broadcast_to(ownf[r, q, source : source + 1, :], (8, 128))
                    high = jnp.broadcast_to(ownf[r, q, source + 1 : source + 2, :], (8, 128))
                    block = jnp.concatenate([low, high], axis=0).astype(BF16) * masks[t]
                    masked[q, t, 8 * a : 8 * a + 16, start : start + 128] = block

    def planes(rows, q, t, r):
        start = 2 * OWN * t
        return rows[r, q, start : start + 16, :], rows[r, q, start + OWN : start + OWN + 16, :]

    def data(rows, q, t, first, last):
        real, imag = [], []
        for r in range(first, last):
            p, v = planes(rows, q, t, r)
            real += [p, v]
            imag += [-v, p]
        return jnp.concatenate([jnp.concatenate(real, axis=1), jnp.concatenate(imag, axis=1)], axis=0).astype(BF16)

    def multiply(left, right):
        return lax.dot_general(left, right, (((1,), (1,)), ((), ())), preferred_element_type=F32)

    def place(q, t, out):
        for a in range(OWN):
            acc[a, q, 6 * t : 6 * t + 8, :] += out[8 * a : 8 * a + 8]

    def squares(q, t, first, last):
        total = None
        for r in range(first, last):
            p, v = planes(othf, q, t, r)
            term = jnp.concatenate([p * p, v * v], axis=1)
            total = term if total is None else total + term
        return total

    acc[...] = jnp.zeros_like(acc)
    power[...] = jnp.zeros_like(power)
    pad = 2 * OWN * TILES
    ownf[:, :, pad:, :] = jnp.zeros((5, QUARTERS, 8, 128), F32)
    othf[:, :, pad:, :] = jnp.zeros((5, QUARTERS, 8, 128), F32)
    nothing = jnp.zeros((32, 256 * TOP), BF16)

    def own_quarter(q, carry):
        @pl.when(core == 0)
        def _():
            local_top(q).wait()
            to_core0(q).wait_recv()

        @pl.when(core == 1)
        def _():
            local_mid(q).wait()
            to_core1(q).wait_recv()

        lay(own, ownf, q, RIM, 5)
        for t in range(TILES):
            expand(q, t, RIM, 5)
        for t in range(TILES):
            right = jnp.concatenate([data(ownf, q, t, RIM, 5), nothing], axis=0)
            place(q, t, multiply(masked[q, t, :, 256 * RIM :], right))
        return carry

    lax.fori_loop(0, QUARTERS, own_quarter, 0)

    loads[2].wait()
    loads[3].wait()
    phi[...] = jnp.zeros_like(phi)
    for s in range(2):
        rows = screens[s]
        picked = jnp.where(core == 0, rows[:, 0, :], rows[:, 1, :])
        phi[16 * s : 16 * s + OWN, :] = picked
    trig[0] = jnp.cos(phi[...])
    trig[1] = jnp.sin(phi[...])

    tab_chip.wait_recv()

    @pl.when(both(core == 1, has_down))
    def _():
        for c in range(2):
            tab_up(c).wait_recv()

    slot = iota((16, 128), 0)
    own_index = jnp.where(slot < OWN, OWN * y + slot, -9)
    oth_index = jnp.where(slot < OWN, OWN * (y + 1) + slot, -9)
    partners[...] = jnp.full((16, 128), -1, I32)
    for b in range(2):
        partners[ACQ * b : ACQ * (b + 1), :] = othtab[b, 0:ACQ, :]
    other_table = partners[...]
    for a in range(OWN):
        k = a
        cos_a, sin_a = trig[0, k : k + 1, :], trig[1, k : k + 1, :]
        line = owntab[a // ACQ, a % ACQ : a % ACQ + 1, :]
        theirs = jnp.where(other_table == OWN * y + a, 1.0, 0.0)
        hits = (
            jnp.where(line == own_index, 1.0, 0.0),
            jnp.where(core == 0, jnp.where(line == oth_index, 1.0, 0.0), theirs),
        )
        for s in range(2):
            w = jnp.sum(hits[s], axis=1, keepdims=True)
            cos_b, sin_b = trig[0, 16 * s : 16 * s + 16, :], trig[1, 16 * s : 16 * s + 16, :]
            turn[s, a, 0] = w * (cos_a * cos_b + sin_a * sin_b)
            turn[s, a, 1] = w * (sin_a * cos_b - cos_a * sin_b)
            turn[s, a, 2] = jnp.broadcast_to(w, (16, 128))

    def other_quarter(q, carry):
        @pl.when(both(core == 0, has_up))
        def _():
            for b in range(2):
                wide(q, 0, 0, TOP, oth, RIM, me, oth_recv.at[q, b]).wait_recv()

        @pl.when(both(core == 1, has_down))
        def _():
            for b in range(2):
                wide(q, 1, TOP, MID, oth, 0, me, oth_recv.at[q, b]).wait_recv()

        lay(oth, othf, q, RIM, 5)
        for t in range(TILES):
            right = jnp.concatenate([nothing, data(othf, q, t, RIM, 5)], axis=0)
            place(q, t, multiply(masked[q, t, :, 256 * RIM :], right))
            square[q, t] = squares(q, t, RIM, 5)
        return carry

    lax.fori_loop(0, QUARTERS, other_quarter, 0)

    @pl.when(has_rim)
    def _():
        for b in range(2):
            rim_copy(0, b, own, me, az).wait_recv()

        @pl.when(has_up)
        def _():
            for b in range(2):
                rim_copy(1, b, oth, me, az).wait_recv()

    def split(v):
        high = v.astype(BF16)
        return [high, (v - high.astype(F32)).astype(BF16)]

    def rim_quarter(q, carry):
        lay(own, ownf, q, 0, RIM)
        lay(oth, othf, q, 0, RIM)
        for t in range(TILES):
            expand(q, t, 0, RIM)
        for t in range(TILES):
            right = jnp.concatenate([data(ownf, q, t, 0, RIM), data(othf, q, t, 0, RIM)], axis=0)
            place(q, t, multiply(masked[q, t, :, : 256 * RIM], right))
            total = jnp.concatenate(split(square[q, t] + squares(q, t, 0, RIM)), axis=0)
            ones = jnp.concatenate([masks[t], masks[t]], axis=1)
            power[q, 6 * t : 6 * t + 8, :] += multiply(ones, total)[0:8]
        return carry

    lax.fori_loop(0, QUARTERS, rim_quarter, 0)

    for a in range(OWN):
        turned[a] = jnp.transpose(acc[a].reshape(128, 64))
    summed = jnp.transpose(power[...].reshape(128, 32))
    othpow[...] = jnp.where(iota((16, 128), 0) < OWN, summed[0:16] + summed[16:32], 1.0)

    mypow[...] = jnp.ones_like(mypow)
    for a in range(OWN):
        mypow[a : a + 1, :] = turned[a, a : a + 1, :]

    first = jnp.where(core == 0, 1.0, 0.0).astype(F32)
    sums[...] = jnp.zeros_like(sums)
    gain = [jnp.zeros((16, 128), F32), jnp.zeros((16, 128), F32)]
    loss = jnp.zeros((16, 128), F32)
    for a in range(OWN):
        k = a
        slopes, misses = [], []
        for s, powers in enumerate((mypow[...], othpow[...])):
            real, imag = turned[a, 32 * s : 32 * s + 16, :], turned[a, 32 * s + 16 : 32 * s + 32, :]
            norm = lax.rsqrt(mypow[k : k + 1, :] * powers + EPSILON)
            cosine, sine = turn[s, a, 0], turn[s, a, 1]
            slope = norm * (imag * cosine - real * sine)
            gain[s] += slope
            slopes.append(slope)
            misses.append(turn[s, a, 2] - norm * (real * cosine + imag * sine))
        loss += misses[1]
        sums[0, k : k + 1, :] = -jnp.sum(slopes[0] + slopes[1], axis=0, keepdims=True)
        sums[1, k : k + 1, :] = jnp.sum(misses[0] + first * misses[1], axis=0, keepdims=True)
    sums[0] += gain[0]
    other_sums[0] = gain[1]
    other_sums[1] = (1.0 - first) * loss
    for b in range(2):
        for f in range(2):
            msg_own[b, 8 * f : 8 * f + ACQ, :] = sums[f, ACQ * b : ACQ * (b + 1), :]
            msg_oth[b, 8 * f : 8 * f + ACQ, :] = other_sums[f, ACQ * b : ACQ * (b + 1), :]
    fin_chip = small(2, msg_own.at[1 - core], fin_own.at[core], 2 * y + 1 - core, 3)
    fin_chip.start()

    def fin_side(b):
        return small(3 + b, msg_oth.at[b], fin_oth.at[core], 2 * side + b, 4 + core)

    @pl.when(has_side)
    def _():
        for b in range(2):
            fin_side(b).start()

    fin_own[core] = msg_own[core]
    fin_chip.wait_recv()

    @pl.when(has_down)
    def _():
        small(3, msg_oth.at[0], fin_oth.at[0], me, 4).wait_recv()

    @pl.when(has_up)
    def _():
        small(3, msg_oth.at[1], fin_oth.at[1], me, 5).wait_recv()

    for j in range(2):
        total = fin_own[j] + fin_oth[j]
        grad_ref[:, j, :] = total[0:ACQ]
        misfit_ref[:, j, :] = total[8 : 8 + ACQ]

    def drain(t, carry):
        @pl.when(has_down)
        def _():
            to_down(t).wait_send()

        @pl.when(has_up)
        def _():
            to_up(t).wait_send()

        @pl.when(core == 0)
        def _():
            to_core1(t).wait_send()

        @pl.when(core == 1)
        def _():
            to_core0(t).wait_send()

        return carry

    lax.fori_loop(0, QUARTERS, drain, 0)

    @pl.when(has_next)
    def _():
        rim_copy(0, core, own, 2 * y, az_next).wait_send()

        @pl.when(has_down)
        def _():
            rim_copy(1, core, oth, 2 * down, az_next).wait_send()

    tab_chip.wait_send()

    @pl.when(has_up)
    def _():
        tab_up(core).wait_send()

    fin_chip.wait_send()

    @pl.when(has_side)
    def _():
        for b in range(2):
            fin_side(b).wait_send()


def local(chips, slabs, complex_slabs, secondaries, pair_counts, phase_screens):
    columns = complex_slabs.shape[3]
    x = jnp.transpose(complex_slabs, (0, 2, 1, 3))
    vmem = pl.BlockSpec(memory_space=pltpu.VMEM)
    hbm = pl.BlockSpec(memory_space=pltpu.HBM)
    out = jax.ShapeDtypeStruct((ACQ, 2, 128), F32)
    return pl.pallas_call(
        functools.partial(kernel, chips, slabs),
        out_shape=(out, out),
        in_specs=[hbm] * 4,
        out_specs=(vmem, vmem),
        scratch_shapes=[
            pltpu.VMEM(secondaries.shape, I32),
            pltpu.SMEM(pair_counts.shape, I32),
            pltpu.VMEM((2, OWN, 2, 128), F32),
            pltpu.VMEM((2, ACQ, 5, 2, columns), BF16),
            pltpu.VMEM((2, ACQ, 5, 2, columns), BF16),
            pltpu.VMEM((5, QUARTERS, 2 * OWN * TILES + 8, 128), F32),
            pltpu.VMEM((5, QUARTERS, 2 * OWN * TILES + 8, 128), F32),
            pltpu.VMEM((QUARTERS, TILES, 8 * OWN, 256 * 5), BF16),
            pltpu.VMEM((OWN, QUARTERS, 32, 64), F32),
            pltpu.VMEM((OWN, 64, 128), F32),
            pltpu.VMEM((QUARTERS, TILES, 16, 256), F32),
            pltpu.VMEM((QUARTERS, 32, 32), F32),
            pltpu.VMEM((8, 128), I32),
            pltpu.VMEM((2, 8, 128), I32),
            pltpu.VMEM((2, 8, 128), I32),
            pltpu.VMEM((16, 128), I32),
            pltpu.VMEM((16, 128), F32),
            pltpu.VMEM((16, 128), F32),
            pltpu.VMEM((32, 128), F32),
            pltpu.VMEM((2, 32, 128), F32),
            pltpu.VMEM((2, OWN, 3, 16, 128), F32),
            pltpu.VMEM((2, 16, 128), F32),
            pltpu.VMEM((2, 16, 128), F32),
            pltpu.VMEM((2, 16, 128), F32),
            pltpu.VMEM((2, 16, 128), F32),
            pltpu.VMEM((2, 16, 128), F32),
            pltpu.VMEM((2, 16, 128), F32),
            pltpu.SemaphoreType.DMA((4,)),
            pltpu.SemaphoreType.DMA((QUARTERS,)),
            pltpu.SemaphoreType.DMA((QUARTERS, 3)),
            pltpu.SemaphoreType.DMA((2,)),
            pltpu.SemaphoreType.DMA((QUARTERS, 2)),
            pltpu.SemaphoreType.DMA((QUARTERS,)),
            pltpu.SemaphoreType.DMA((2, 2)),
            pltpu.SemaphoreType.DMA((5,)),
            pltpu.SemaphoreType.DMA((6,)),
        ],
        compiler_params=pltpu.CompilerParams(
            collective_id=0, has_side_effects=True, vmem_limit_bytes=56 * 1024 * 1024
        ),
    )(x, secondaries, pair_counts, phase_screens)


def solution(mesh):
    return jax.shard_map(
        functools.partial(local, mesh.shape["acq"] // 2, mesh.shape["az"]),
        mesh=mesh,
        in_specs=(P("acq", None, "az", None), P("acq", None), P("acq"), P(None, "az", None)),
        out_specs=(P("acq", "az", None), P("acq", "az", None)),
        check_vma=False,
    )
```

```python
import functools

import jax
import jax.numpy as jnp
from jax import lax
from jax.experimental import pallas as pl
from jax.experimental.pallas import tpu as pltpu
from jax.sharding import PartitionSpec as P

EPSILON = 1e-6
MESH = pl.DeviceIdType.MESH
F32, BF16, I32 = jnp.float32, jnp.bfloat16, jnp.int32

ACQ = 6
OWN = 12
QUARTERS, TILES, QUARTER = 4, 5, 640
RUN = 8
TOP, MID, RIM = 3, 5, 2


def iota(shape, dim):
    return lax.broadcasted_iota(I32, shape, dim)


def kernel(
    chips, slabs,
    x_hbm, sec_hbm, cnt_hbm, screens_hbm,
    grad_ref, misfit_ref,
    secs, cnts, screens, own, oth, ownf, othf, masked, acc, turned, square, power,
    mytab, owntab, othtab, partners, mypow, othpow, phi, trig, turn, sums, other_sums, msg_own, msg_oth, fin_own, fin_oth,
    load_sem, local_sem, send_sem, rim_send, chip_send, oth_recv, own_recv, rim_recv, small_send, small_recv,
):
    me = lax.axis_index("acq")
    az = lax.axis_index("az")
    y, core = me // 2, me % 2
    up, down = jnp.minimum(y + 1, chips - 1), jnp.maximum(y - 1, 0)
    az_next, az_prev = jnp.minimum(az + 1, slabs - 1), jnp.maximum(az - 1, 0)
    has_up, has_down = y < chips - 1, y > 0
    has_next, has_prev = az < slabs - 1, az > 0
    side = jnp.where(core == 0, up, down)
    has_side = jnp.logical_or(jnp.logical_and(core == 0, has_up), jnp.logical_and(core == 1, has_down))
    has_rim = jnp.logical_and(core == 0, has_prev)
    both = jnp.logical_and

    loads = [
        pltpu.make_async_copy(sec_hbm, secs, load_sem.at[0]),
        pltpu.make_async_copy(cnt_hbm, cnts, load_sem.at[1]),
        pltpu.make_async_copy(screens_hbm.at[pl.ds(OWN * y, OWN)], screens.at[0], load_sem.at[2]),
        pltpu.make_async_copy(screens_hbm.at[pl.ds(OWN * side, OWN)], screens.at[1], load_sem.at[3]),
    ]
    for load in loads:
        load.start()

    def columns(q):
        return pl.ds(pl.multiple_of(QUARTER * q, 128), QUARTER)

    local_top = pltpu.make_async_copy(x_hbm.at[:, pl.ds(0, TOP)], own.at[0, :, pl.ds(RIM, TOP)], local_sem)
    local_mid = pltpu.make_async_copy(x_hbm.at[:, pl.ds(TOP, MID)], own.at[1], local_sem)

    @pl.when(core == 0)
    def _():
        local_top.start()

    @pl.when(core == 1)
    def _():
        local_mid.start()

    fin_oth[...] = jnp.zeros_like(fin_oth)
    msg_own[...] = jnp.zeros_like(msg_own)
    msg_oth[...] = jnp.zeros_like(msg_oth)
    othtab[...] = jnp.full((2, 8, 128), -1, I32)

    barrier = pltpu.get_barrier_semaphore()

    def greet(a, z):
        pl.semaphore_signal(barrier, inc=1, device_id=(a, z), device_id_type=MESH)

    greet(2 * y + 1 - core, az)

    @pl.when(has_up)
    def _():
        for c in range(2):
            greet(2 * up + c, az)

    @pl.when(has_down)
    def _():
        for c in range(2):
            greet(2 * down + c, az)

    @pl.when(has_rim)
    def _():
        for c in range(2):
            greet(2 * y + c, az_prev)

        @pl.when(has_up)
        def _():
            for c in range(2):
                greet(2 * up + c, az_prev)

    def flag(condition):
        return jnp.where(condition, 1, 0)

    expected = 1 + 2 * flag(has_up) + 2 * flag(has_down) + flag(has_next) + flag(both(has_next, has_down))

    @pl.when(both(core == 0, jnp.logical_not(has_prev)))
    def _():
        own[:, :, 0:RIM] = jnp.zeros((2, ACQ, RIM, 2, QUARTERS * QUARTER), BF16)
        oth[:, :, 0:RIM] = jnp.zeros((2, ACQ, RIM, 2, QUARTERS * QUARTER), BF16)

    @pl.when(jnp.logical_not(has_side))
    def _():
        oth[...] = jnp.zeros_like(oth)

    def small(k, src, dst, a, sem):
        return pltpu.make_async_remote_copy(
            src_ref=src, dst_ref=dst, send_sem=small_send.at[k], recv_sem=small_recv.at[sem],
            device_id=(a, az), device_id_type=MESH,
        )

    def wide(q, k, first, rows, buffer, start, a, sem):
        return pltpu.make_async_remote_copy(
            src_ref=x_hbm.at[:, pl.ds(first, rows), :, columns(q)],
            dst_ref=buffer.at[core, :, pl.ds(start, rows), :, columns(q)],
            send_sem=send_sem.at[q, k], recv_sem=sem,
            device_id=(a, az), device_id_type=MESH,
        )

    def to_down(q):
        return wide(q, 0, 0, TOP, oth, RIM, 2 * down, oth_recv.at[q, core])

    def to_up(q):
        return wide(q, 1, TOP, MID, oth, 0, 2 * up + 1, oth_recv.at[q, core])

    def chip_copy(first, rows, start, a):
        return pltpu.make_async_remote_copy(
            src_ref=x_hbm.at[:, pl.ds(first, rows)], dst_ref=own.at[core, :, pl.ds(start, rows)],
            send_sem=chip_send, recv_sem=own_recv, device_id=(a, az), device_id_type=MESH,
        )

    to_core1 = chip_copy(TOP, MID, 0, 2 * y + 1)
    to_core0 = chip_copy(0, TOP, RIM, 2 * y)

    def rim_copy(k, block, buffer, a, z):
        return pltpu.make_async_remote_copy(
            src_ref=x_hbm.at[:, pl.ds(TOP + MID, RIM)],
            dst_ref=buffer.at[block, :, pl.ds(0, RIM)],
            send_sem=rim_send.at[k], recv_sem=rim_recv.at[k, block],
            device_id=(a, z), device_id_type=MESH,
        )

    pl.semaphore_wait(barrier, expected)

    @pl.when(has_next)
    def _():
        rim_copy(0, core, own, 2 * y, az_next).start()

        @pl.when(has_down)
        def _():
            rim_copy(1, core, oth, 2 * down, az_next).start()

    @pl.when(core == 0)
    def _():
        to_core1.start()

    @pl.when(core == 1)
    def _():
        to_core0.start()

    @pl.when(has_up)
    def _():
        for q in range(QUARTERS):
            to_up(q).start()

    rim_first = both(has_next, az % RUN == RUN - 1)

    @pl.when(rim_first)
    def _():
        rim_copy(0, core, own, 2 * y, az_next).wait_send()

        @pl.when(has_down)
        def _():
            rim_copy(1, core, oth, 2 * down, az_next).wait_send()

    @pl.when(has_down)
    def _():
        for q in range(QUARTERS):
            to_down(q).start()

    loads[0].wait()
    loads[1].wait()
    mytab[...] = jnp.full((8, 128), -1, I32)
    mytab[0:ACQ, 0:10] = secs[...]
    slots = jnp.zeros((8, 128), I32)
    for i in range(ACQ):
        slots = jnp.where(iota((8, 128), 0) == i, cnts[i], slots)
    mytab[...] = jnp.where(iota((8, 128), 1) < slots, mytab[...], -1)
    owntab[core] = mytab[...]

    tab_chip = small(0, mytab, owntab.at[core], 2 * y + 1 - core, 0)
    tab_chip.start()

    def tab_up(c):
        return small(1, mytab, othtab.at[c], 2 * up + 1, 1 + c)

    @pl.when(has_up)
    def _():
        tab_up(core).start()

    def lay(buffer, rows, q, first, last):
        for r in range(first, last):
            for a in range(OWN):
                v = buffer[a // ACQ, a % ACQ, r, :, columns(q)].astype(F32)
                for t in range(TILES):
                    rows[r, q, pl.ds(2 * OWN * t + a, 2, stride=OWN), :] = v[:, 128 * t : 128 * (t + 1)]

    def cell_mask(t):
        column = iota((16, 128), 1) + 128 * t
        slot = ((column * 3277) >> 16) - 6 * t
        return jnp.where(slot == (iota((16, 128), 0) & 7), 1.0, 0.0).astype(BF16)

    masks = [cell_mask(t) for t in range(TILES)]

    def expand(q, t, first, last):
        parts = []
        for r in range(first, last):
            for c in range(2):
                lines = []
                for a in range(OWN):
                    source = 2 * OWN * t + OWN * c + a
                    lines.append(jnp.broadcast_to(ownf[r, q, source : source + 1, :], (8, 128)))
                parts.append(jnp.concatenate(lines, axis=0).astype(BF16) * jnp.concatenate([masks[t]] * (OWN // 2), axis=0))
        return jnp.concatenate(parts, axis=1)

    def planes(rows, q, t, r):
        start = 2 * OWN * t
        return rows[r, q, start : start + 16, :], rows[r, q, start + OWN : start + OWN + 16, :]

    def data(rows, q, t, first, last):
        real, imag = [], []
        for r in range(first, last):
            p, v = planes(rows, q, t, r)
            real += [p, v]
            imag += [-v, p]
        return jnp.concatenate([jnp.concatenate(real, axis=1), jnp.concatenate(imag, axis=1)], axis=0).astype(BF16)

    def multiply(left, right):
        return lax.dot_general(left, right, (((1,), (1,)), ((), ())), preferred_element_type=F32)

    even = iota((8, 128), 1) < 64

    def place(q, t, left, right):
        out = multiply(left, jnp.concatenate([right, right], axis=0))
        for p in range(OWN // 2):
            acc[p, q, 6 * t : 6 * t + 8, :] += jnp.where(even, out[16 * p : 16 * p + 8], out[16 * p + 8 : 16 * p + 16])

    def squares(q, t, first, last):
        total = None
        for r in range(first, last):
            p, v = planes(othf, q, t, r)
            term = jnp.concatenate([p * p, v * v], axis=1)
            total = term if total is None else total + term
        return total

    acc[...] = jnp.zeros_like(acc)
    power[...] = jnp.zeros_like(power)
    square[...] = jnp.zeros_like(square)
    pad = 2 * OWN * TILES
    ownf[:, :, pad:, :] = jnp.zeros((5, QUARTERS, 8, 128), F32)
    othf[:, :, pad:, :] = jnp.zeros((5, QUARTERS, 8, 128), F32)
    nothing = jnp.zeros((32, 256 * TOP), BF16)

    @pl.when(core == 0)
    def _():
        local_top.wait()
        to_core0.wait_recv()

    @pl.when(core == 1)
    def _():
        local_mid.wait()
        to_core1.wait_recv()

    def own_quarter(q, carry):
        lay(own, ownf, q, RIM, 5)
        for t in range(TILES):
            left = expand(q, t, RIM, 5)
            masked[q, t] = left
            place(q, t, left, jnp.concatenate([data(ownf, q, t, RIM, 5), nothing], axis=0))
        return carry

    lax.fori_loop(0, QUARTERS, own_quarter, 0)

    loads[2].wait()
    loads[3].wait()
    phi[...] = jnp.zeros_like(phi)
    for s in range(2):
        rows = screens[s]
        picked = jnp.where(core == 0, rows[:, 0, :], rows[:, 1, :])
        phi[16 * s : 16 * s + OWN, :] = picked
    trig[0] = jnp.cos(phi[...])
    trig[1] = jnp.sin(phi[...])

    tab_chip.wait_recv()

    @pl.when(both(core == 1, has_down))
    def _():
        for c in range(2):
            tab_up(c).wait_recv()

    slot = iota((16, 128), 0)
    own_index = jnp.where(slot < OWN, OWN * y + slot, -9)
    oth_index = jnp.where(slot < OWN, OWN * (y + 1) + slot, -9)
    partners[...] = jnp.full((16, 128), -1, I32)
    for b in range(2):
        partners[ACQ * b : ACQ * (b + 1), :] = othtab[b, 0:ACQ, :]
    other_table = partners[...]
    for a in range(OWN):
        k = a
        cos_a, sin_a = trig[0, k : k + 1, :], trig[1, k : k + 1, :]
        line = owntab[a // ACQ, a % ACQ : a % ACQ + 1, :]
        theirs = jnp.where(other_table == OWN * y + a, 1.0, 0.0)
        hits = (
            jnp.where(line == own_index, 1.0, 0.0),
            jnp.where(core == 0, jnp.where(line == oth_index, 1.0, 0.0), theirs),
        )
        for s in range(2):
            w = jnp.sum(hits[s], axis=1, keepdims=True)
            cos_b, sin_b = trig[0, 16 * s : 16 * s + 16, :], trig[1, 16 * s : 16 * s + 16, :]
            turn[s, a, 0] = w * (cos_a * cos_b + sin_a * sin_b)
            turn[s, a, 1] = w * (sin_a * cos_b - cos_a * sin_b)
            turn[s, a, 2] = jnp.broadcast_to(w, (16, 128))

    def rim_phase():
        @pl.when(has_rim)
        def _():
            for b in range(2):
                rim_copy(0, b, own, me, az).wait_recv()

            @pl.when(has_up)
            def _():
                for b in range(2):
                    rim_copy(1, b, oth, me, az).wait_recv()

        def rim_half(h, carry):
            for q in (2 * h, 2 * h + 1):
                lay(own, ownf, q, 0, RIM)
                lay(oth, othf, q, 0, RIM)
            for q in (2 * h, 2 * h + 1):
                for t in range(TILES):
                    right = jnp.concatenate([data(ownf, q, t, 0, RIM), data(othf, q, t, 0, RIM)], axis=0)
                    place(q, t, expand(q, t, 0, RIM), right)
                    square[q, t] += squares(q, t, 0, RIM)
            return carry

        lax.fori_loop(0, QUARTERS // 2, rim_half, 0)

    rim_last = jnp.logical_or(core == 1, az % RUN == 0)

    @pl.when(jnp.logical_not(rim_last))
    def _():
        rim_phase()

    def other_quarter(q, carry):
        @pl.when(both(core == 0, has_up))
        def _():
            for b in range(2):
                wide(q, 0, 0, TOP, oth, RIM, me, oth_recv.at[q, b]).wait_recv()

        @pl.when(both(core == 1, has_down))
        def _():
            for b in range(2):
                wide(q, 1, TOP, MID, oth, 0, me, oth_recv.at[q, b]).wait_recv()

        lay(oth, othf, q, RIM, 5)
        for t in range(TILES):
            right = jnp.concatenate([nothing, data(othf, q, t, RIM, 5)], axis=0)
            place(q, t, masked[q, t], right)
            square[q, t] += squares(q, t, RIM, 5)
        return carry

    lax.fori_loop(0, QUARTERS, other_quarter, 0)

    @pl.when(rim_last)
    def _():
        rim_phase()

    def split(v):
        high = v.astype(BF16)
        return [high, (v - high.astype(F32)).astype(BF16)]

    for q in range(QUARTERS):
        for t in range(TILES):
            ones = jnp.concatenate([masks[t], masks[t]], axis=1)
            power[q, 6 * t : 6 * t + 8, :] += multiply(ones, jnp.concatenate(split(square[q, t]), axis=0))[0:8]

    for p in range(OWN // 2):
        turned[2 * p : 2 * p + 2] = jnp.transpose(acc[p].reshape(128, 128)).reshape(2, 64, 128)
    summed = jnp.transpose(power[...].reshape(128, 32))
    othpow[...] = jnp.where(iota((16, 128), 0) < OWN, summed[0:16] + summed[16:32], 1.0)

    mypow[...] = jnp.ones_like(mypow)
    for a in range(OWN):
        mypow[a : a + 1, :] = turned[a, a : a + 1, :]

    first = jnp.where(core == 0, 1.0, 0.0).astype(F32)
    sums[...] = jnp.zeros_like(sums)
    gain = [jnp.zeros((16, 128), F32), jnp.zeros((16, 128), F32)]
    loss = jnp.zeros((16, 128), F32)
    for a in range(OWN):
        k = a
        slopes, misses = [], []
        for s, powers in enumerate((mypow[...], othpow[...])):
            real, imag = turned[a, 32 * s : 32 * s + 16, :], turned[a, 32 * s + 16 : 32 * s + 32, :]
            norm = lax.rsqrt(mypow[k : k + 1, :] * powers + EPSILON)
            cosine, sine = turn[s, a, 0], turn[s, a, 1]
            slope = norm * (imag * cosine - real * sine)
            gain[s] += slope
            slopes.append(slope)
            misses.append(turn[s, a, 2] - norm * (real * cosine + imag * sine))
        loss += misses[1]
        sums[0, k : k + 1, :] = -jnp.sum(slopes[0] + slopes[1], axis=0, keepdims=True)
        sums[1, k : k + 1, :] = jnp.sum(misses[0] + first * misses[1], axis=0, keepdims=True)
    sums[0] += gain[0]
    other_sums[0] = gain[1]
    other_sums[1] = (1.0 - first) * loss
    for b in range(2):
        for f in range(2):
            msg_own[b, 8 * f : 8 * f + ACQ, :] = sums[f, ACQ * b : ACQ * (b + 1), :]
            msg_oth[b, 8 * f : 8 * f + ACQ, :] = other_sums[f, ACQ * b : ACQ * (b + 1), :]
    fin_chip = small(2, msg_own.at[1 - core], fin_own.at[core], 2 * y + 1 - core, 3)
    fin_chip.start()

    def fin_side(b):
        return small(3 + b, msg_oth.at[b], fin_oth.at[core], 2 * side + b, 4 + core)

    @pl.when(has_side)
    def _():
        for b in range(2):
            fin_side(b).start()

    fin_own[core] = msg_own[core]

    @pl.when(has_down)
    def _():
        for q in range(QUARTERS):
            to_down(q).wait_send()

    @pl.when(has_up)
    def _():
        for q in range(QUARTERS):
            to_up(q).wait_send()

        tab_up(core).wait_send()

    @pl.when(core == 0)
    def _():
        to_core1.wait_send()

    @pl.when(core == 1)
    def _():
        to_core0.wait_send()

    @pl.when(both(has_next, jnp.logical_not(rim_first)))
    def _():
        rim_copy(0, core, own, 2 * y, az_next).wait_send()

        @pl.when(has_down)
        def _():
            rim_copy(1, core, oth, 2 * down, az_next).wait_send()

    tab_chip.wait_send()
    fin_chip.wait_send()

    @pl.when(has_side)
    def _():
        for b in range(2):
            fin_side(b).wait_send()

    fin_chip.wait_recv()

    @pl.when(has_down)
    def _():
        small(3, msg_oth.at[0], fin_oth.at[0], me, 4).wait_recv()

    @pl.when(has_up)
    def _():
        small(3, msg_oth.at[1], fin_oth.at[1], me, 5).wait_recv()

    for j in range(2):
        total = fin_own[j] + fin_oth[j]
        grad_ref[:, j, :] = total[0:ACQ]
        misfit_ref[:, j, :] = total[8 : 8 + ACQ]


def local(chips, slabs, complex_slabs, secondaries, pair_counts, phase_screens):
    columns = complex_slabs.shape[3]
    x = jnp.transpose(complex_slabs, (0, 2, 1, 3))
    vmem = pl.BlockSpec(memory_space=pltpu.VMEM)
    hbm = pl.BlockSpec(memory_space=pltpu.HBM)
    out = jax.ShapeDtypeStruct((ACQ, 2, 128), F32)
    return pl.pallas_call(
        functools.partial(kernel, chips, slabs),
        out_shape=(out, out),
        in_specs=[hbm] * 4,
        out_specs=(vmem, vmem),
        scratch_shapes=[
            pltpu.VMEM(secondaries.shape, I32),
            pltpu.SMEM(pair_counts.shape, I32),
            pltpu.VMEM((2, OWN, 2, 128), F32),
            pltpu.VMEM((2, ACQ, 5, 2, columns), BF16),
            pltpu.VMEM((2, ACQ, 5, 2, columns), BF16),
            pltpu.VMEM((5, QUARTERS, 2 * OWN * TILES + 8, 128), F32),
            pltpu.VMEM((5, QUARTERS, 2 * OWN * TILES + 8, 128), F32),
            pltpu.VMEM((QUARTERS, TILES, 8 * OWN, 256 * TOP), BF16),
            pltpu.VMEM((OWN // 2, QUARTERS, 32, 128), F32),
            pltpu.VMEM((OWN, 64, 128), F32),
            pltpu.VMEM((QUARTERS, TILES, 16, 256), F32),
            pltpu.VMEM((QUARTERS, 32, 32), F32),
            pltpu.VMEM((8, 128), I32),
            pltpu.VMEM((2, 8, 128), I32),
            pltpu.VMEM((2, 8, 128), I32),
            pltpu.VMEM((16, 128), I32),
            pltpu.VMEM((16, 128), F32),
            pltpu.VMEM((16, 128), F32),
            pltpu.VMEM((32, 128), F32),
            pltpu.VMEM((2, 32, 128), F32),
            pltpu.VMEM((2, OWN, 3, 16, 128), F32),
            pltpu.VMEM((2, 16, 128), F32),
            pltpu.VMEM((2, 16, 128), F32),
            pltpu.VMEM((2, 16, 128), F32),
            pltpu.VMEM((2, 16, 128), F32),
            pltpu.VMEM((2, 16, 128), F32),
            pltpu.VMEM((2, 16, 128), F32),
            pltpu.SemaphoreType.DMA((4,)),
            pltpu.SemaphoreType.DMA,
            pltpu.SemaphoreType.DMA((QUARTERS, 2)),
            pltpu.SemaphoreType.DMA((2,)),
            pltpu.SemaphoreType.DMA,
            pltpu.SemaphoreType.DMA((QUARTERS, 2)),
            pltpu.SemaphoreType.DMA,
            pltpu.SemaphoreType.DMA((2, 2)),
            pltpu.SemaphoreType.DMA((5,)),
            pltpu.SemaphoreType.DMA((6,)),
        ],
        compiler_params=pltpu.CompilerParams(
            collective_id=0, has_side_effects=True, vmem_limit_bytes=56 * 1024 * 1024
        ),
    )(x, secondaries, pair_counts, phase_screens)


def solution(mesh):
    return jax.shard_map(
        functools.partial(local, mesh.shape["acq"] // 2, mesh.shape["az"]),
        mesh=mesh,
        in_specs=(P("acq", None, "az", None), P("acq", None), P("acq"), P(None, "az", None)),
        out_specs=(P("acq", "az", None), P("acq", "az", None)),
        check_vma=False,
    )
```

```python
import functools

import jax
import jax.numpy as jnp
from jax import lax
from jax.experimental import pallas as pl
from jax.experimental.pallas import tpu as pltpu
from jax.sharding import PartitionSpec as P

EPSILON = 1e-6
MESH = pl.DeviceIdType.MESH
F32, BF16, I32 = jnp.float32, jnp.bfloat16, jnp.int32

ACQ = 6
OWN = 12
QUARTERS, TILES, QUARTER = 4, 5, 640
RUN = 8
TOP, MID, RIM = 3, 5, 2


def iota(shape, dim):
    return lax.broadcasted_iota(I32, shape, dim)


def kernel(
    chips, slabs,
    x_hbm, sec_hbm, cnt_hbm, screens_hbm,
    out_ref,
    secs, cnts, screens, own, oth, ownf, othf, masked, acc, turned, power,
    mytab, owntab, othtab, partners, mypow, othpow, phi, trig, turn, sums, other_sums, msg_own, msg_oth, fin_own, fin_oth,
    load_sem, local_sem, send_sem, rim_send, chip_send, oth_recv, own_recv, rim_recv, small_send, small_recv,
):
    me = lax.axis_index("acq")
    az = lax.axis_index("az")
    y, core = me // 2, me % 2
    up, down = jnp.minimum(y + 1, chips - 1), jnp.maximum(y - 1, 0)
    az_next, az_prev = jnp.minimum(az + 1, slabs - 1), jnp.maximum(az - 1, 0)
    has_up, has_down = y < chips - 1, y > 0
    has_next, has_prev = az < slabs - 1, az > 0
    side = jnp.where(core == 0, up, down)
    has_side = jnp.logical_or(jnp.logical_and(core == 0, has_up), jnp.logical_and(core == 1, has_down))
    has_rim = jnp.logical_and(core == 0, has_prev)
    both = jnp.logical_and

    loads = [
        pltpu.make_async_copy(sec_hbm, secs, load_sem.at[0]),
        pltpu.make_async_copy(cnt_hbm, cnts, load_sem.at[1]),
        pltpu.make_async_copy(screens_hbm.at[pl.ds(OWN * y, OWN)], screens.at[0], load_sem.at[2]),
        pltpu.make_async_copy(screens_hbm.at[pl.ds(OWN * side, OWN)], screens.at[1], load_sem.at[3]),
    ]
    for load in loads:
        load.start()

    def columns(q):
        return pl.ds(pl.multiple_of(QUARTER * q, 128), QUARTER)

    local_top = pltpu.make_async_copy(x_hbm.at[:, pl.ds(0, TOP)], own.at[0, :, pl.ds(RIM, TOP)], local_sem)
    local_mid = pltpu.make_async_copy(x_hbm.at[:, pl.ds(TOP, MID)], own.at[1], local_sem)

    @pl.when(core == 0)
    def _():
        local_top.start()

    @pl.when(core == 1)
    def _():
        local_mid.start()

    fin_oth[...] = jnp.zeros_like(fin_oth)
    msg_own[...] = jnp.zeros_like(msg_own)
    msg_oth[...] = jnp.zeros_like(msg_oth)
    othtab[...] = jnp.full((2, 8, 128), -1, I32)

    barrier = pltpu.get_barrier_semaphore()

    def greet(a, z):
        pl.semaphore_signal(barrier, inc=1, device_id=(a, z), device_id_type=MESH)

    greet(2 * y + 1 - core, az)

    @pl.when(has_up)
    def _():
        for c in range(2):
            greet(2 * up + c, az)

    @pl.when(has_down)
    def _():
        for c in range(2):
            greet(2 * down + c, az)

    @pl.when(has_rim)
    def _():
        for c in range(2):
            greet(2 * y + c, az_prev)

        @pl.when(has_up)
        def _():
            for c in range(2):
                greet(2 * up + c, az_prev)

    def flag(condition):
        return jnp.where(condition, 1, 0)

    expected = 1 + 2 * flag(has_up) + 2 * flag(has_down) + flag(has_next) + flag(both(has_next, has_down))

    @pl.when(jnp.logical_not(has_side))
    def _():
        oth[...] = jnp.zeros_like(oth)

    def small(k, src, dst, a, sem):
        return pltpu.make_async_remote_copy(
            src_ref=src, dst_ref=dst, send_sem=small_send.at[k], recv_sem=small_recv.at[sem],
            device_id=(a, az), device_id_type=MESH,
        )

    def wide(q, k, first, rows, buffer, start, a, sem):
        return pltpu.make_async_remote_copy(
            src_ref=x_hbm.at[:, pl.ds(first, rows), :, columns(q)],
            dst_ref=buffer.at[core, :, pl.ds(start, rows), :, columns(q)],
            send_sem=send_sem.at[q, k], recv_sem=sem,
            device_id=(a, az), device_id_type=MESH,
        )

    def to_down(q):
        return wide(q, 0, 0, TOP, oth, RIM, 2 * down, oth_recv.at[q, core])

    def to_up(q):
        return wide(q, 1, TOP, MID, oth, 0, 2 * up + 1, oth_recv.at[q, core])

    def chip_copy(first, rows, start, a):
        return pltpu.make_async_remote_copy(
            src_ref=x_hbm.at[:, pl.ds(first, rows)], dst_ref=own.at[core, :, pl.ds(start, rows)],
            send_sem=chip_send, recv_sem=own_recv, device_id=(a, az), device_id_type=MESH,
        )

    to_core1 = chip_copy(TOP, MID, 0, 2 * y + 1)
    to_core0 = chip_copy(0, TOP, RIM, 2 * y)

    def rim_copy(k, q, block, buffer, a, z):
        return pltpu.make_async_remote_copy(
            src_ref=x_hbm.at[:, pl.ds(TOP + MID, RIM), :, columns(q)],
            dst_ref=buffer.at[block, :, pl.ds(0, RIM), :, columns(q)],
            send_sem=rim_send.at[k, q], recv_sem=rim_recv.at[k, block, q],
            device_id=(a, z), device_id_type=MESH,
        )

    def own_rim(q):
        return rim_copy(0, q, core, own, 2 * y, az_next)

    def oth_rim(q):
        return rim_copy(1, q, core, oth, 2 * down, az_next)

    def wait_rims():
        for q in range(QUARTERS):
            own_rim(q).wait_send()

        @pl.when(has_down)
        def _():
            for q in range(QUARTERS):
                oth_rim(q).wait_send()

    pl.semaphore_wait(barrier, expected)

    @pl.when(both(has_next, has_down))
    def _():
        for q in range(QUARTERS):
            own_rim(q).start()
            oth_rim(q).start()

    @pl.when(both(has_next, jnp.logical_not(has_down)))
    def _():
        for q in range(QUARTERS):
            own_rim(q).start()

    @pl.when(core == 0)
    def _():
        to_core1.start()

    @pl.when(core == 1)
    def _():
        to_core0.start()

    @pl.when(has_up)
    def _():
        for q in range(QUARTERS):
            to_up(q).start()

    rim_first = both(has_next, az % RUN == RUN - 1)

    @pl.when(rim_first)
    def _():
        wait_rims()

    @pl.when(has_down)
    def _():
        for q in range(QUARTERS):
            to_down(q).start()

    loads[0].wait()
    loads[1].wait()
    mytab[...] = jnp.full((8, 128), -1, I32)
    mytab[0:ACQ, 0:10] = secs[...]
    slots = jnp.zeros((8, 128), I32)
    for i in range(ACQ):
        slots = jnp.where(iota((8, 128), 0) == i, cnts[i], slots)
    mytab[...] = jnp.where(iota((8, 128), 1) < slots, mytab[...], -1)
    owntab[core] = mytab[...]

    tab_chip = small(0, mytab, owntab.at[core], 2 * y + 1 - core, 0)
    tab_chip.start()

    def tab_up(c):
        return small(1, mytab, othtab.at[c], 2 * up + 1, 1 + c)

    @pl.when(has_up)
    def _():
        tab_up(core).start()

    def lay(buffer, rows, q, first, last):
        for r in range(first, last):
            for a in range(OWN):
                v = buffer[a // ACQ, a % ACQ, r, :, columns(q)].astype(F32)
                for t in range(TILES):
                    rows[r, q, pl.ds(2 * OWN * t + a, 2, stride=OWN), :] = v[:, 128 * t : 128 * (t + 1)]

    def cell_mask(t):
        column = iota((16, 128), 1) + 128 * t
        slot = ((column * 3277) >> 16) - 6 * t
        return jnp.where(slot == (iota((16, 128), 0) & 7), 1.0, 0.0).astype(BF16)

    masks = [cell_mask(t) for t in range(TILES)]

    def expand(q, t, first, last):
        parts = []
        for r in range(first, last):
            for c in range(2):
                lines = []
                for a in range(OWN):
                    source = 2 * OWN * t + OWN * c + a
                    lines.append(jnp.broadcast_to(ownf[r, q, source : source + 1, :], (8, 128)))
                parts.append(jnp.concatenate(lines, axis=0).astype(BF16) * jnp.concatenate([masks[t]] * (OWN // 2), axis=0))
        return jnp.concatenate(parts, axis=1)

    def planes(rows, q, t, r):
        start = 2 * OWN * t
        return rows[r, q, start : start + 16, :], rows[r, q, start + OWN : start + OWN + 16, :]

    def data(rows, q, t, first, last):
        real, imag = [], []
        for r in range(first, last):
            p, v = planes(rows, q, t, r)
            real += [p, v]
            imag += [-v, p]
        return jnp.concatenate([jnp.concatenate(real, axis=1), jnp.concatenate(imag, axis=1)], axis=0).astype(BF16)

    def multiply(left, right):
        return lax.dot_general(left, right, (((1,), (1,)), ((), ())), preferred_element_type=F32)

    even = iota((8, 128), 1) < 64

    def place(q, t, left, right):
        out = multiply(left, jnp.concatenate([right, right], axis=0))
        for p in range(OWN // 2):
            acc[p, q, 6 * t : 6 * t + 8, :] += jnp.where(even, out[16 * p : 16 * p + 8], out[16 * p + 8 : 16 * p + 16])

    def split(v):
        high = v.astype(BF16)
        return [high, (v - high.astype(F32)).astype(BF16)]

    def add_power(q, t, first, last):
        total = None
        for r in range(first, last):
            p, v = planes(othf, q, t, r)
            term = jnp.concatenate([p * p, v * v], axis=1)
            total = term if total is None else total + term
        ones = jnp.concatenate([masks[t], masks[t]], axis=1)
        power[q, 6 * t : 6 * t + 8, :] += multiply(ones, jnp.concatenate(split(total), axis=0))[0:8]

    acc[...] = jnp.zeros_like(acc)
    power[...] = jnp.zeros_like(power)
    pad = 2 * OWN * TILES
    ownf[:, :, pad:, :] = jnp.zeros((5, QUARTERS, 8, 128), F32)
    othf[:, :, pad:, :] = jnp.zeros((5, QUARTERS, 8, 128), F32)
    nothing = jnp.zeros((32, 256 * TOP), BF16)

    @pl.when(core == 0)
    def _():
        local_top.wait()
        to_core0.wait_recv()

    @pl.when(core == 1)
    def _():
        local_mid.wait()
        to_core1.wait_recv()

    def own_quarter(q, carry):
        lay(own, ownf, q, RIM, 5)
        for t in range(TILES):
            left = expand(q, t, RIM, 5)
            masked[q, t] = left
            place(q, t, left, jnp.concatenate([data(ownf, q, t, RIM, 5), nothing], axis=0))
        return carry

    lax.fori_loop(0, QUARTERS, own_quarter, 0)

    loads[2].wait()
    loads[3].wait()
    phi[...] = jnp.zeros_like(phi)
    for s in range(2):
        rows = screens[s]
        picked = jnp.where(core == 0, rows[:, 0, :], rows[:, 1, :])
        phi[16 * s : 16 * s + OWN, :] = picked
    trig[0] = jnp.cos(phi[...])
    trig[1] = jnp.sin(phi[...])

    tab_chip.wait_recv()

    @pl.when(both(core == 1, has_down))
    def _():
        for c in range(2):
            tab_up(c).wait_recv()

    slot = iota((16, 128), 0)
    own_index = jnp.where(slot < OWN, OWN * y + slot, -9)
    oth_index = jnp.where(slot < OWN, OWN * (y + 1) + slot, -9)
    partners[...] = jnp.full((16, 128), -1, I32)
    for b in range(2):
        partners[ACQ * b : ACQ * (b + 1), :] = othtab[b, 0:ACQ, :]
    other_table = partners[...]
    for a in range(OWN):
        k = a
        cos_a, sin_a = trig[0, k : k + 1, :], trig[1, k : k + 1, :]
        line = owntab[a // ACQ, a % ACQ : a % ACQ + 1, :]
        theirs = jnp.where(other_table == OWN * y + a, 1.0, 0.0)
        hits = (
            jnp.where(line == own_index, 1.0, 0.0),
            jnp.where(core == 0, jnp.where(line == oth_index, 1.0, 0.0), theirs),
        )
        for s in range(2):
            w = jnp.sum(hits[s], axis=1, keepdims=True)
            cos_b, sin_b = trig[0, 16 * s : 16 * s + 16, :], trig[1, 16 * s : 16 * s + 16, :]
            turn[s, a, 0] = w * (cos_a * cos_b + sin_a * sin_b)
            turn[s, a, 1] = w * (sin_a * cos_b - cos_a * sin_b)
            turn[s, a, 2] = jnp.broadcast_to(w, (16, 128))

    def rim_part(q):
        @pl.when(core == 0)
        def _():
            for b in range(2):
                rim_copy(0, q, b, own, me, az).wait_recv()

        @pl.when(both(core == 0, has_up))
        def _():
            for b in range(2):
                rim_copy(1, q, b, oth, me, az).wait_recv()

        lay(own, ownf, q, 0, RIM)
        lay(oth, othf, q, 0, RIM)
        for t in range(TILES):
            right = jnp.concatenate([data(ownf, q, t, 0, RIM), data(othf, q, t, 0, RIM)], axis=0)
            place(q, t, expand(q, t, 0, RIM), right)
            add_power(q, t, 0, RIM)

    def main_part(q):
        @pl.when(both(core == 0, has_up))
        def _():
            for b in range(2):
                wide(q, 0, 0, TOP, oth, RIM, me, oth_recv.at[q, b]).wait_recv()

        @pl.when(both(core == 1, has_down))
        def _():
            for b in range(2):
                wide(q, 1, TOP, MID, oth, 0, me, oth_recv.at[q, b]).wait_recv()

        lay(oth, othf, q, RIM, 5)
        for t in range(TILES):
            right = jnp.concatenate([nothing, data(othf, q, t, RIM, 5)], axis=0)
            place(q, t, masked[q, t], right)
            add_power(q, t, RIM, 5)

    rim_late = az % RUN == 0
    has_first = jnp.logical_or(core == 1, has_prev)

    def step(i, carry):
        half = i // QUARTERS
        rim = jnp.where(core == 1, i % 2, jnp.where(rim_late, half, 1 - half))
        q = jnp.where(core == 1, i // 2, i % QUARTERS)

        @pl.when(both(rim == 1, has_first))
        def _():
            rim_part(q)

        @pl.when(rim == 0)
        def _():
            main_part(q)

        return carry

    lax.fori_loop(0, 2 * QUARTERS, step, 0)

    for p in range(OWN // 2):
        turned[2 * p : 2 * p + 2] = jnp.transpose(acc[p].reshape(128, 128)).reshape(2, 64, 128)
    summed = jnp.transpose(power[...].reshape(128, 32))
    othpow[...] = jnp.where(iota((16, 128), 0) < OWN, summed[0:16] + summed[16:32], 1.0)

    mypow[...] = jnp.ones_like(mypow)
    for a in range(OWN):
        mypow[a : a + 1, :] = turned[a, a : a + 1, :]

    first = jnp.where(core == 0, 1.0, 0.0).astype(F32)
    sums[...] = jnp.zeros_like(sums)
    gain = [jnp.zeros((16, 128), F32), jnp.zeros((16, 128), F32)]
    loss = jnp.zeros((16, 128), F32)
    for a in range(OWN):
        k = a
        slopes, misses = [], []
        for s, powers in enumerate((mypow[...], othpow[...])):
            real, imag = turned[a, 32 * s : 32 * s + 16, :], turned[a, 32 * s + 16 : 32 * s + 32, :]
            norm = lax.rsqrt(mypow[k : k + 1, :] * powers + EPSILON)
            cosine, sine = turn[s, a, 0], turn[s, a, 1]
            slope = norm * (imag * cosine - real * sine)
            gain[s] += slope
            slopes.append(slope)
            misses.append(turn[s, a, 2] - norm * (real * cosine + imag * sine))
        loss += misses[1]
        sums[0, k : k + 1, :] = -jnp.sum(slopes[0] + slopes[1], axis=0, keepdims=True)
        sums[1, k : k + 1, :] = jnp.sum(misses[0] + first * misses[1], axis=0, keepdims=True)
    sums[0] += gain[0]
    other_sums[0] = gain[1]
    other_sums[1] = (1.0 - first) * loss
    for b in range(2):
        for f in range(2):
            msg_own[b, 8 * f : 8 * f + ACQ, :] = sums[f, ACQ * b : ACQ * (b + 1), :]
            msg_oth[b, 8 * f : 8 * f + ACQ, :] = other_sums[f, ACQ * b : ACQ * (b + 1), :]
    fin_chip = small(2, msg_own.at[1 - core], fin_own.at[core], 2 * y + 1 - core, 3)
    fin_chip.start()

    def fin_side(b):
        return small(3 + b, msg_oth.at[b], fin_oth.at[core], 2 * side + b, 4 + core)

    @pl.when(has_side)
    def _():
        for b in range(2):
            fin_side(b).start()

    fin_own[core] = msg_own[core]

    @pl.when(has_down)
    def _():
        for q in range(QUARTERS):
            to_down(q).wait_send()

    @pl.when(has_up)
    def _():
        for q in range(QUARTERS):
            to_up(q).wait_send()

        tab_up(core).wait_send()

    @pl.when(core == 0)
    def _():
        to_core1.wait_send()

    @pl.when(core == 1)
    def _():
        to_core0.wait_send()

    @pl.when(both(has_next, jnp.logical_not(rim_first)))
    def _():
        wait_rims()

    tab_chip.wait_send()
    fin_chip.wait_send()

    @pl.when(has_side)
    def _():
        for b in range(2):
            fin_side(b).wait_send()

    fin_chip.wait_recv()

    @pl.when(has_down)
    def _():
        small(3, msg_oth.at[0], fin_oth.at[0], me, 4).wait_recv()

    @pl.when(has_up)
    def _():
        small(3, msg_oth.at[1], fin_oth.at[1], me, 5).wait_recv()

    for j in range(2):
        total = fin_own[j] + fin_oth[j]
        out_ref[0, :, j, :] = total[0:ACQ]
        out_ref[1, :, j, :] = total[8 : 8 + ACQ]


def local(chips, slabs, complex_slabs, secondaries, pair_counts, phase_screens):
    columns = complex_slabs.shape[3]
    x = jnp.transpose(complex_slabs, (0, 2, 1, 3))
    vmem = pl.BlockSpec(memory_space=pltpu.VMEM)
    hbm = pl.BlockSpec(memory_space=pltpu.HBM)
    out = jax.ShapeDtypeStruct((2, ACQ, 2, 128), F32)
    both = pl.pallas_call(
        functools.partial(kernel, chips, slabs),
        out_shape=out,
        in_specs=[hbm] * 4,
        out_specs=vmem,
        scratch_shapes=[
            pltpu.VMEM(secondaries.shape, I32),
            pltpu.SMEM(pair_counts.shape, I32),
            pltpu.VMEM((2, OWN, 2, 128), F32),
            pltpu.VMEM((2, ACQ, 5, 2, columns), BF16),
            pltpu.VMEM((2, ACQ, 5, 2, columns), BF16),
            pltpu.VMEM((5, QUARTERS, 2 * OWN * TILES + 8, 128), F32),
            pltpu.VMEM((5, QUARTERS, 2 * OWN * TILES + 8, 128), F32),
            pltpu.VMEM((QUARTERS, TILES, 8 * OWN, 256 * TOP), BF16),
            pltpu.VMEM((OWN // 2, QUARTERS, 32, 128), F32),
            pltpu.VMEM((OWN, 64, 128), F32),
            pltpu.VMEM((QUARTERS, 32, 32), F32),
            pltpu.VMEM((8, 128), I32),
            pltpu.VMEM((2, 8, 128), I32),
            pltpu.VMEM((2, 8, 128), I32),
            pltpu.VMEM((16, 128), I32),
            pltpu.VMEM((16, 128), F32),
            pltpu.VMEM((16, 128), F32),
            pltpu.VMEM((32, 128), F32),
            pltpu.VMEM((2, 32, 128), F32),
            pltpu.VMEM((2, OWN, 3, 16, 128), F32),
            pltpu.VMEM((2, 16, 128), F32),
            pltpu.VMEM((2, 16, 128), F32),
            pltpu.VMEM((2, 16, 128), F32),
            pltpu.VMEM((2, 16, 128), F32),
            pltpu.VMEM((2, 16, 128), F32),
            pltpu.VMEM((2, 16, 128), F32),
            pltpu.SemaphoreType.DMA((4,)),
            pltpu.SemaphoreType.DMA,
            pltpu.SemaphoreType.DMA((QUARTERS, 2)),
            pltpu.SemaphoreType.DMA((2, QUARTERS)),
            pltpu.SemaphoreType.DMA,
            pltpu.SemaphoreType.DMA((QUARTERS, 2)),
            pltpu.SemaphoreType.DMA,
            pltpu.SemaphoreType.DMA((2, 2, QUARTERS)),
            pltpu.SemaphoreType.DMA((5,)),
            pltpu.SemaphoreType.DMA((6,)),
        ],
        compiler_params=pltpu.CompilerParams(
            collective_id=0, has_side_effects=True, vmem_limit_bytes=56 * 1024 * 1024
        ),
    )(x, secondaries, pair_counts, phase_screens)
    return both[0], both[1]


def solution(mesh):
    return jax.shard_map(
        functools.partial(local, mesh.shape["acq"] // 2, mesh.shape["az"]),
        mesh=mesh,
        in_specs=(P("acq", None, "az", None), P("acq", None), P("acq"), P(None, "az", None)),
        out_specs=(P("acq", "az", None), P("acq", "az", None)),
        check_vma=False,
    )
```

```python
import functools

import jax
import jax.numpy as jnp
from jax import lax
from jax.experimental import pallas as pl
from jax.experimental.pallas import tpu as pltpu
from jax.sharding import PartitionSpec as P

EPSILON = 1e-6
MESH = pl.DeviceIdType.MESH
F32, BF16, I32 = jnp.float32, jnp.bfloat16, jnp.int32

ACQ = 6
OWN = 12
QUARTERS, TILES, QUARTER = 4, 5, 640
FIRST, SECOND = (0, 1), (2, 3)
RUN = 8
TOP, MID, RIM = 3, 5, 2


def iota(shape, dim):
    return lax.broadcasted_iota(I32, shape, dim)


def kernel(
    chips, slabs,
    x_hbm, sec_hbm, cnt_hbm, screens_hbm,
    out_ref,
    secs, cnts, screens, own, oth, ownf, othf, masked, acc, turned, power,
    mytab, owntab, othtab, partners, mypow, othpow, phi, trig, turn, sums, other_sums, msg_own, msg_oth, fin_own, fin_oth,
    load_sem, local_sem, send_sem, rim_send, chip_send, oth_recv, own_recv, rim_recv, small_send, small_recv,
):
    me = lax.axis_index("acq")
    az = lax.axis_index("az")
    y, core = me // 2, me % 2
    up, down = jnp.minimum(y + 1, chips - 1), jnp.maximum(y - 1, 0)
    az_next, az_prev = jnp.minimum(az + 1, slabs - 1), jnp.maximum(az - 1, 0)
    has_up, has_down = y < chips - 1, y > 0
    has_next, has_prev = az < slabs - 1, az > 0
    side = jnp.where(core == 0, up, down)
    has_side = jnp.logical_or(jnp.logical_and(core == 0, has_up), jnp.logical_and(core == 1, has_down))
    has_rim = jnp.logical_and(core == 0, has_prev)
    both = jnp.logical_and

    loads = [
        pltpu.make_async_copy(sec_hbm, secs, load_sem.at[0]),
        pltpu.make_async_copy(cnt_hbm, cnts, load_sem.at[1]),
        pltpu.make_async_copy(screens_hbm.at[pl.ds(OWN * y, OWN)], screens.at[0], load_sem.at[2]),
        pltpu.make_async_copy(screens_hbm.at[pl.ds(OWN * side, OWN)], screens.at[1], load_sem.at[3]),
    ]
    for load in loads:
        load.start()

    def columns(q):
        return pl.ds(pl.multiple_of(QUARTER * q, 128), QUARTER)

    local_top = pltpu.make_async_copy(x_hbm.at[:, pl.ds(0, TOP)], own.at[0, :, pl.ds(RIM, TOP)], local_sem)
    local_mid = pltpu.make_async_copy(x_hbm.at[:, pl.ds(TOP, MID)], own.at[1], local_sem)

    @pl.when(core == 0)
    def _():
        local_top.start()

    @pl.when(core == 1)
    def _():
        local_mid.start()

    fin_oth[...] = jnp.zeros_like(fin_oth)
    msg_own[...] = jnp.zeros_like(msg_own)
    msg_oth[...] = jnp.zeros_like(msg_oth)
    othtab[...] = jnp.full((2, 8, 128), -1, I32)

    barrier = pltpu.get_barrier_semaphore()

    def greet(a, z):
        pl.semaphore_signal(barrier, inc=1, device_id=(a, z), device_id_type=MESH)

    greet(2 * y + 1 - core, az)

    @pl.when(has_up)
    def _():
        for c in range(2):
            greet(2 * up + c, az)

    @pl.when(has_down)
    def _():
        for c in range(2):
            greet(2 * down + c, az)

    @pl.when(has_rim)
    def _():
        for c in range(2):
            greet(2 * y + c, az_prev)

        @pl.when(has_up)
        def _():
            for c in range(2):
                greet(2 * up + c, az_prev)

    def flag(condition):
        return jnp.where(condition, 1, 0)

    expected = 1 + 2 * flag(has_up) + 2 * flag(has_down) + flag(has_next) + flag(both(has_next, has_down))

    @pl.when(jnp.logical_not(has_side))
    def _():
        oth[...] = jnp.zeros_like(oth)

    def small(k, src, dst, a, sem):
        return pltpu.make_async_remote_copy(
            src_ref=src, dst_ref=dst, send_sem=small_send.at[k], recv_sem=small_recv.at[sem],
            device_id=(a, az), device_id_type=MESH,
        )

    def wide(q, k, first, rows, buffer, start, a, sem):
        return pltpu.make_async_remote_copy(
            src_ref=x_hbm.at[:, pl.ds(first, rows), :, columns(q)],
            dst_ref=buffer.at[core, :, pl.ds(start, rows), :, columns(q)],
            send_sem=send_sem.at[q, k], recv_sem=sem,
            device_id=(a, az), device_id_type=MESH,
        )

    def to_down(q):
        return wide(q, 0, 0, TOP, oth, RIM, 2 * down, oth_recv.at[q, core])

    def to_up(q):
        return wide(q, 1, TOP, MID, oth, 0, 2 * up + 1, oth_recv.at[q, core])

    def chip_copy(first, rows, start, a):
        return pltpu.make_async_remote_copy(
            src_ref=x_hbm.at[:, pl.ds(first, rows)], dst_ref=own.at[core, :, pl.ds(start, rows)],
            send_sem=chip_send, recv_sem=own_recv, device_id=(a, az), device_id_type=MESH,
        )

    to_core1 = chip_copy(TOP, MID, 0, 2 * y + 1)
    to_core0 = chip_copy(0, TOP, RIM, 2 * y)

    def rim_copy(k, q, block, buffer, a, z):
        return pltpu.make_async_remote_copy(
            src_ref=x_hbm.at[:, pl.ds(TOP + MID, RIM), :, columns(q)],
            dst_ref=buffer.at[block, :, pl.ds(0, RIM), :, columns(q)],
            send_sem=rim_send.at[k, q], recv_sem=rim_recv.at[k, block, q],
            device_id=(a, z), device_id_type=MESH,
        )

    def own_rim(q):
        return rim_copy(0, q, core, own, 2 * y, az_next)

    def oth_rim(q):
        return rim_copy(1, q, core, oth, 2 * down, az_next)

    def start_rims(quarters):
        @pl.when(has_down)
        def _():
            for q in quarters:
                own_rim(q).start()
                oth_rim(q).start()

        @pl.when(jnp.logical_not(has_down))
        def _():
            for q in quarters:
                own_rim(q).start()

    def wait_rims(quarters):
        for q in quarters:
            own_rim(q).wait_send()

        @pl.when(has_down)
        def _():
            for q in quarters:
                oth_rim(q).wait_send()

    pl.semaphore_wait(barrier, expected)

    @pl.when(has_next)
    def _():
        start_rims(FIRST)

    @pl.when(has_next)
    def _():
        start_rims(SECOND)

    @pl.when(core == 0)
    def _():
        to_core1.start()

    @pl.when(core == 1)
    def _():
        to_core0.start()

    @pl.when(has_up)
    def _():
        for q in FIRST:
            to_up(q).start()

    @pl.when(has_down)
    def _():
        for q in FIRST:
            to_down(q).start()

    loads[0].wait()
    loads[1].wait()
    mytab[...] = jnp.full((8, 128), -1, I32)
    mytab[0:ACQ, 0:10] = secs[...]
    slots = jnp.zeros((8, 128), I32)
    for i in range(ACQ):
        slots = jnp.where(iota((8, 128), 0) == i, cnts[i], slots)
    mytab[...] = jnp.where(iota((8, 128), 1) < slots, mytab[...], -1)
    owntab[core] = mytab[...]

    tab_chip = small(0, mytab, owntab.at[core], 2 * y + 1 - core, 0)
    tab_chip.start()

    def tab_up(c):
        return small(1, mytab, othtab.at[c], 2 * up + 1, 1 + c)

    @pl.when(has_up)
    def _():
        tab_up(core).start()

    def lay(buffer, rows, q, first, last):
        for r in range(first, last):
            for a in range(OWN):
                v = buffer[a // ACQ, a % ACQ, r, :, columns(q)].astype(F32)
                for t in range(TILES):
                    rows[r, q, pl.ds(2 * OWN * t + a, 2, stride=OWN), :] = v[:, 128 * t : 128 * (t + 1)]

    def cell_mask(t):
        column = iota((16, 128), 1) + 128 * t
        slot = ((column * 3277) >> 16) - 6 * t
        return jnp.where(slot == (iota((16, 128), 0) & 7), 1.0, 0.0).astype(BF16)

    masks = [cell_mask(t) for t in range(TILES)]

    def expand(q, t, first, last):
        parts = []
        for r in range(first, last):
            for c in range(2):
                lines = []
                for a in range(OWN):
                    source = 2 * OWN * t + OWN * c + a
                    lines.append(jnp.broadcast_to(ownf[r, q, source : source + 1, :], (8, 128)))
                parts.append(jnp.concatenate(lines, axis=0).astype(BF16) * jnp.concatenate([masks[t]] * (OWN // 2), axis=0))
        return jnp.concatenate(parts, axis=1)

    def planes(rows, q, t, r):
        start = 2 * OWN * t
        return rows[r, q, start : start + 16, :], rows[r, q, start + OWN : start + OWN + 16, :]

    def data(rows, q, t, first, last):
        real, imag = [], []
        for r in range(first, last):
            p, v = planes(rows, q, t, r)
            real += [p, v]
            imag += [-v, p]
        return jnp.concatenate([jnp.concatenate(real, axis=1), jnp.concatenate(imag, axis=1)], axis=0).astype(BF16)

    def multiply(left, right):
        return lax.dot_general(left, right, (((1,), (1,)), ((), ())), preferred_element_type=F32)

    even = iota((8, 128), 1) < 64

    def place(q, t, left, right):
        out = multiply(left, jnp.concatenate([right, right], axis=0))
        for p in range(OWN // 2):
            acc[p, q, 6 * t : 6 * t + 8, :] += jnp.where(even, out[16 * p : 16 * p + 8], out[16 * p + 8 : 16 * p + 16])

    def split(v):
        high = v.astype(BF16)
        return [high, (v - high.astype(F32)).astype(BF16)]

    def add_power(q, t, first, last):
        total = None
        for r in range(first, last):
            p, v = planes(othf, q, t, r)
            term = jnp.concatenate([p * p, v * v], axis=1)
            total = term if total is None else total + term
        ones = jnp.concatenate([masks[t], masks[t]], axis=1)
        power[q, 6 * t : 6 * t + 8, :] += multiply(ones, jnp.concatenate(split(total), axis=0))[0:8]

    acc[...] = jnp.zeros_like(acc)
    power[...] = jnp.zeros_like(power)
    pad = 2 * OWN * TILES
    ownf[:, :, pad:, :] = jnp.zeros((5, QUARTERS, 8, 128), F32)
    othf[:, :, pad:, :] = jnp.zeros((5, QUARTERS, 8, 128), F32)
    nothing = jnp.zeros((32, 256 * TOP), BF16)

    @pl.when(core == 0)
    def _():
        local_top.wait()
        to_core0.wait_recv()

    @pl.when(core == 1)
    def _():
        local_mid.wait()
        to_core1.wait_recv()

    def own_quarter(q, carry):
        lay(own, ownf, q, RIM, 5)
        for t in range(TILES):
            left = expand(q, t, RIM, 5)
            masked[q, t] = left
            place(q, t, left, jnp.concatenate([data(ownf, q, t, RIM, 5), nothing], axis=0))
        return carry

    lax.fori_loop(0, 2, own_quarter, 0)

    lax.fori_loop(2, QUARTERS, own_quarter, 0)

    @pl.when(has_up)
    def _():
        for q in FIRST:
            to_up(q).wait_send()
        for q in SECOND:
            to_up(q).start()

    @pl.when(has_down)
    def _():
        for q in FIRST:
            to_down(q).wait_send()
        for q in SECOND:
            to_down(q).start()

    loads[2].wait()
    loads[3].wait()
    phi[...] = jnp.zeros_like(phi)
    for s in range(2):
        rows = screens[s]
        picked = jnp.where(core == 0, rows[:, 0, :], rows[:, 1, :])
        phi[16 * s : 16 * s + OWN, :] = picked
    trig[0] = jnp.cos(phi[...])
    trig[1] = jnp.sin(phi[...])

    tab_chip.wait_recv()

    @pl.when(both(core == 1, has_down))
    def _():
        for c in range(2):
            tab_up(c).wait_recv()

    slot = iota((16, 128), 0)
    own_index = jnp.where(slot < OWN, OWN * y + slot, -9)
    oth_index = jnp.where(slot < OWN, OWN * (y + 1) + slot, -9)
    partners[...] = jnp.full((16, 128), -1, I32)
    for b in range(2):
        partners[ACQ * b : ACQ * (b + 1), :] = othtab[b, 0:ACQ, :]
    other_table = partners[...]
    for a in range(OWN):
        k = a
        cos_a, sin_a = trig[0, k : k + 1, :], trig[1, k : k + 1, :]
        line = owntab[a // ACQ, a % ACQ : a % ACQ + 1, :]
        theirs = jnp.where(other_table == OWN * y + a, 1.0, 0.0)
        hits = (
            jnp.where(line == own_index, 1.0, 0.0),
            jnp.where(core == 0, jnp.where(line == oth_index, 1.0, 0.0), theirs),
        )
        for s in range(2):
            w = jnp.sum(hits[s], axis=1, keepdims=True)
            cos_b, sin_b = trig[0, 16 * s : 16 * s + 16, :], trig[1, 16 * s : 16 * s + 16, :]
            turn[s, a, 0] = w * (cos_a * cos_b + sin_a * sin_b)
            turn[s, a, 1] = w * (sin_a * cos_b - cos_a * sin_b)
            turn[s, a, 2] = jnp.broadcast_to(w, (16, 128))

    def rim_part(h):
        pair = (2 * h, 2 * h + 1)

        @pl.when(core == 0)
        def _():
            for q in pair:
                for b in range(2):
                    rim_copy(0, q, b, own, me, az).wait_recv()

        @pl.when(both(core == 0, has_up))
        def _():
            for q in pair:
                for b in range(2):
                    rim_copy(1, q, b, oth, me, az).wait_recv()

        for q in pair:
            lay(own, ownf, q, 0, RIM)
            lay(oth, othf, q, 0, RIM)
        for q in pair:
            for t in range(TILES):
                right = jnp.concatenate([data(ownf, q, t, 0, RIM), data(othf, q, t, 0, RIM)], axis=0)
                place(q, t, expand(q, t, 0, RIM), right)
                add_power(q, t, 0, RIM)

    def main_part(q):
        @pl.when(both(core == 0, has_up))
        def _():
            for b in range(2):
                wide(q, 0, 0, TOP, oth, RIM, me, oth_recv.at[q, b]).wait_recv()

        @pl.when(both(core == 1, has_down))
        def _():
            for b in range(2):
                wide(q, 1, TOP, MID, oth, 0, me, oth_recv.at[q, b]).wait_recv()

        lay(oth, othf, q, RIM, 5)
        for t in range(TILES):
            right = jnp.concatenate([nothing, data(othf, q, t, RIM, 5)], axis=0)
            place(q, t, masked[q, t], right)
            add_power(q, t, RIM, 5)

    rim_late = az % RUN == 0
    has_first = jnp.logical_or(core == 1, has_prev)

    def step(i, carry):
        rim = jnp.where(core == 1, i % 3 // 2, jnp.where(rim_late, i // 4, 1 - jnp.minimum(i // 2, 1)))
        h = jnp.where(core == 1, i // 3, i % 2)
        q = jnp.where(core == 1, i - i // 3, jnp.where(rim_late, i, i - 2))

        @pl.when(both(rim == 1, has_first))
        def _():
            rim_part(h)

        @pl.when(rim == 0)
        def _():
            main_part(q)

        return carry

    lax.fori_loop(0, QUARTERS + 2, step, 0)

    for p in range(OWN // 2):
        turned[2 * p : 2 * p + 2] = jnp.transpose(acc[p].reshape(128, 128)).reshape(2, 64, 128)
    summed = jnp.transpose(power[...].reshape(128, 32))
    othpow[...] = jnp.where(iota((16, 128), 0) < OWN, summed[0:16] + summed[16:32], 1.0)

    mypow[...] = jnp.ones_like(mypow)
    for a in range(OWN):
        mypow[a : a + 1, :] = turned[a, a : a + 1, :]

    first = jnp.where(core == 0, 1.0, 0.0).astype(F32)
    sums[...] = jnp.zeros_like(sums)
    gain = [jnp.zeros((16, 128), F32), jnp.zeros((16, 128), F32)]
    loss = jnp.zeros((16, 128), F32)
    for a in range(OWN):
        k = a
        slopes, misses = [], []
        for s, powers in enumerate((mypow[...], othpow[...])):
            real, imag = turned[a, 32 * s : 32 * s + 16, :], turned[a, 32 * s + 16 : 32 * s + 32, :]
            norm = lax.rsqrt(mypow[k : k + 1, :] * powers + EPSILON)
            cosine, sine = turn[s, a, 0], turn[s, a, 1]
            slope = norm * (imag * cosine - real * sine)
            gain[s] += slope
            slopes.append(slope)
            misses.append(turn[s, a, 2] - norm * (real * cosine + imag * sine))
        loss += misses[1]
        sums[0, k : k + 1, :] = -jnp.sum(slopes[0] + slopes[1], axis=0, keepdims=True)
        sums[1, k : k + 1, :] = jnp.sum(misses[0] + first * misses[1], axis=0, keepdims=True)
    sums[0] += gain[0]
    other_sums[0] = gain[1]
    other_sums[1] = (1.0 - first) * loss
    for b in range(2):
        for f in range(2):
            msg_own[b, 8 * f : 8 * f + ACQ, :] = sums[f, ACQ * b : ACQ * (b + 1), :]
            msg_oth[b, 8 * f : 8 * f + ACQ, :] = other_sums[f, ACQ * b : ACQ * (b + 1), :]
    fin_chip = small(2, msg_own.at[1 - core], fin_own.at[core], 2 * y + 1 - core, 3)
    fin_chip.start()

    def fin_side(b):
        return small(3 + b, msg_oth.at[b], fin_oth.at[core], 2 * side + b, 4 + core)

    @pl.when(has_side)
    def _():
        for b in range(2):
            fin_side(b).start()

    fin_own[core] = msg_own[core]

    @pl.when(has_down)
    def _():
        for q in SECOND:
            to_down(q).wait_send()

    @pl.when(has_up)
    def _():
        for q in SECOND:
            to_up(q).wait_send()

        tab_up(core).wait_send()

    @pl.when(core == 0)
    def _():
        to_core1.wait_send()

    @pl.when(core == 1)
    def _():
        to_core0.wait_send()

    @pl.when(has_next)
    def _():
        wait_rims(FIRST + SECOND)

    tab_chip.wait_send()
    fin_chip.wait_send()

    @pl.when(has_side)
    def _():
        for b in range(2):
            fin_side(b).wait_send()

    fin_chip.wait_recv()

    @pl.when(has_down)
    def _():
        small(3, msg_oth.at[0], fin_oth.at[0], me, 4).wait_recv()

    @pl.when(has_up)
    def _():
        small(3, msg_oth.at[1], fin_oth.at[1], me, 5).wait_recv()

    for j in range(2):
        total = fin_own[j] + fin_oth[j]
        out_ref[0, :, j, :] = total[0:ACQ]
        out_ref[1, :, j, :] = total[8 : 8 + ACQ]


def local(chips, slabs, complex_slabs, secondaries, pair_counts, phase_screens):
    columns = complex_slabs.shape[3]
    x = jnp.transpose(complex_slabs, (0, 2, 1, 3))
    vmem = pl.BlockSpec(memory_space=pltpu.VMEM)
    hbm = pl.BlockSpec(memory_space=pltpu.HBM)
    out = jax.ShapeDtypeStruct((2, ACQ, 2, 128), F32)
    both = pl.pallas_call(
        functools.partial(kernel, chips, slabs),
        out_shape=out,
        in_specs=[hbm] * 4,
        out_specs=vmem,
        scratch_shapes=[
            pltpu.VMEM(secondaries.shape, I32),
            pltpu.SMEM(pair_counts.shape, I32),
            pltpu.VMEM((2, OWN, 2, 128), F32),
            pltpu.VMEM((2, ACQ, 5, 2, columns), BF16),
            pltpu.VMEM((2, ACQ, 5, 2, columns), BF16),
            pltpu.VMEM((5, QUARTERS, 2 * OWN * TILES + 8, 128), F32),
            pltpu.VMEM((5, QUARTERS, 2 * OWN * TILES + 8, 128), F32),
            pltpu.VMEM((QUARTERS, TILES, 8 * OWN, 256 * TOP), BF16),
            pltpu.VMEM((OWN // 2, QUARTERS, 32, 128), F32),
            pltpu.VMEM((OWN, 64, 128), F32),
            pltpu.VMEM((QUARTERS, 32, 32), F32),
            pltpu.VMEM((8, 128), I32),
            pltpu.VMEM((2, 8, 128), I32),
            pltpu.VMEM((2, 8, 128), I32),
            pltpu.VMEM((16, 128), I32),
            pltpu.VMEM((16, 128), F32),
            pltpu.VMEM((16, 128), F32),
            pltpu.VMEM((32, 128), F32),
            pltpu.VMEM((2, 32, 128), F32),
            pltpu.VMEM((2, OWN, 3, 16, 128), F32),
            pltpu.VMEM((2, 16, 128), F32),
            pltpu.VMEM((2, 16, 128), F32),
            pltpu.VMEM((2, 16, 128), F32),
            pltpu.VMEM((2, 16, 128), F32),
            pltpu.VMEM((2, 16, 128), F32),
            pltpu.VMEM((2, 16, 128), F32),
            pltpu.SemaphoreType.DMA((4,)),
            pltpu.SemaphoreType.DMA,
            pltpu.SemaphoreType.DMA((QUARTERS, 2)),
            pltpu.SemaphoreType.DMA((2, QUARTERS)),
            pltpu.SemaphoreType.DMA,
            pltpu.SemaphoreType.DMA((QUARTERS, 2)),
            pltpu.SemaphoreType.DMA,
            pltpu.SemaphoreType.DMA((2, 2, QUARTERS)),
            pltpu.SemaphoreType.DMA((5,)),
            pltpu.SemaphoreType.DMA((6,)),
        ],
        compiler_params=pltpu.CompilerParams(
            collective_id=0, has_side_effects=True, vmem_limit_bytes=56 * 1024 * 1024
        ),
    )(x, secondaries, pair_counts, phase_screens)
    return both[0], both[1]


def solution(mesh):
    return jax.shard_map(
        functools.partial(local, mesh.shape["acq"] // 2, mesh.shape["az"]),
        mesh=mesh,
        in_specs=(P("acq", None, "az", None), P("acq", None), P("acq"), P(None, "az", None)),
        out_specs=(P("acq", "az", None), P("acq", "az", None)),
        check_vma=False,
    )
```
